128 devices in a mesh: row: 8 (over x_lo, z), col: 16 (over x_hi, y, core).
Axes of the slice: x: 4 (x_hi: 2, x_lo: 2; x = x_hi * 2 + x_lo), y: 4, z: 4, core: 2. Of those that a mesh axis runs over, the one named last changes fastest.
Arguments:
- pair: float32 [512, 512, 128], P('row', 'col')
- token_mask: int32 [512], replicated, may hold values 0 or 1
- norm_gains: float32 [2, 2, 128], replicated, may hold values from 0.1 to 1.9
- norm_biases: float32 [2, 2, 128], replicated, may hold values from -1.5 to 1.5
- in_weights: bfloat16 [2, 128, 640], replicated, may hold values from -0.5 to 0.5
- out_weights: bfloat16 [2, 128, 128], replicated, may hold values from -0.5 to 0.5
Outputs:
- pair_out: float32 [512, 512, 128], P('row', 'col')
The draws below stay inside these ranges and needn't reach their ends.
Inputs may be any that keep to these rules, and one draw needn't show every extreme that they name: `token_mask`: 1 for a token that takes part, 0 for a padding token.
All inputs are finite; a program needn't handle non-finite values.
Results may differ from the reference program's by a relative error of at most 0.0028.
Values may be sent and summed in bfloat16 or wider, within the bound.
A program may use at most 128 MiB of HBM per device.

```python
import jax
import jax.numpy as jnp
from jax import lax

C = 128
TOKENS = 512


def draw_pair(key, part):
    key = jax.random.fold_in(key, 17)
    noise_key, pair_key, chan_key = jax.random.split(key, 3)
    shape_full = (TOKENS, TOKENS, C)
    pair_scale = jnp.exp(jax.random.uniform(pair_key, (TOKENS, TOKENS, 1), jnp.float32, -1.2, 1.2))
    chan_scale = jnp.exp(jax.random.uniform(chan_key, (1, 1, C), jnp.float32, -1.2, 1.2))
    values_drawn = jax.random.normal(noise_key, shape_full, jnp.float32)
    return values_drawn * pair_scale * chan_scale


def place_ends(entries, stream_key, low, top_value):
    spot = [jax.random.randint(jax.random.fold_in(stream_key, axis), (), 0, length) for axis, length in enumerate(entries.shape)]
    longest = entries.shape.index(max(entries.shape))
    beside = spot[:longest] + [(spot[longest] + 1) % entries.shape[longest]] + spot[longest + 1:]
    return entries.at[tuple(spot)].set(low).at[tuple(beside)].set(top_value)


def bell_draw(rng, dims, spread, most, dtype=jnp.bfloat16):
    values = jax.random.normal(rng, dims, jnp.float32) * spread
    return jnp.minimum(jnp.maximum(values, -most), most).astype(dtype)


def setup_inputs(seed: int = 0) -> dict:
    key_list = jax.random.split(jax.random.key(seed), 7)
    return {
        "pair": draw_pair(jax.random.fold_in(key_list[6], 71), 0),
        "token_mask": place_ends((jax.random.randint(key_list[1], (TOKENS,), 0, 8) < 7).astype(jnp.int32), jax.random.fold_in(key_list[1], 1), 0, 1),
        "norm_gains": jnp.clip(1.0 + 0.18 * jax.random.normal(key_list[2], (2, 2, C), jnp.float32), 0.1, 1.9),
        "norm_biases": bell_draw(key_list[3], (2, 2, C), 0.3, 1.5, jnp.float32),
        "in_weights": bell_draw(key_list[4], (2, C, 5 * C), C ** -0.5, 0.5),
        "out_weights": bell_draw(key_list[5], (2, C, C), C ** -0.5, 0.5),
    }


def layer_norm(values, norm_gain, norm_bias):
    average = lax.optimization_barrier(jnp.mean(values, axis=-1, keepdims=True))
    centred = values - average
    variance = lax.optimization_barrier(jnp.mean(centred * centred, axis=-1, keepdims=True))
    return centred * jax.lax.rsqrt(variance + 1e-05) * norm_gain + norm_bias

def triangle_layer(source, pair_mask, norm_gains, norm_biases, weights_in, weights_out, outgoing):
    width = source.shape[-1]
    normed = layer_norm(source, norm_gains[0], norm_biases[0]).astype(jnp.bfloat16)
    projected = jnp.dot(normed.reshape(-1, width), weights_in, preferred_element_type=jnp.float32)
    projected = projected.reshape(source.shape[0], source.shape[1], 5 * width)
    left_side = (projected[..., :width] * jax.nn.sigmoid(projected[..., 2 * width:3 * width]) * pair_mask).astype(jnp.bfloat16)
    right_side = (projected[..., width:2 * width] * jax.nn.sigmoid(projected[..., 3 * width:4 * width]) * pair_mask).astype(jnp.bfloat16)
    out_gate = jax.nn.sigmoid(projected[..., 4 * width:])
    if outgoing:
        combined = jnp.einsum('ikc,jkc->ijc', left_side.astype(jnp.float32), right_side.astype(jnp.float32))
    else:
        combined = jnp.einsum('kic,kjc->ijc', left_side.astype(jnp.float32), right_side.astype(jnp.float32))
    normed_out = layer_norm(combined, norm_gains[1], norm_biases[1]).astype(jnp.bfloat16)
    update = jnp.dot(normed_out.reshape(-1, width), weights_out, preferred_element_type=jnp.float32)
    return source + out_gate * update.reshape(source.shape)

def reference(pair, token_mask, norm_gains, norm_biases, in_weights, out_weights):
    pair_mask = (token_mask[:, None] * token_mask[None, :]).astype(jnp.float32)[:, :, None]
    middle = triangle_layer(pair, pair_mask, norm_gains[0], norm_biases[0], in_weights[0], out_weights[0], True)
    return triangle_layer(middle, pair_mask, norm_gains[1], norm_biases[1], in_weights[1], out_weights[1], False)
```

```python
import functools

import jax
import jax.numpy as jnp
from jax import lax
from jax.experimental import pallas as pl
from jax.experimental.pallas import tpu as pltpu
from jax.sharding import PartitionSpec as P

MESH = pl.DeviceIdType.MESH
F32, BF16 = jnp.float32, jnp.bfloat16
C = 128
ROWS, COLS = 64, 32
NR, NC = 8, 16
ND = NR * NC
CHUNKS = 16
TN = (((0,), (0,)), ((), ()))
NT = (((1,), (1,)), ((), ()))
NN = (((1,), (0,)), ((), ()))


def dot(a, b, dims):
    return lax.dot_general(a, b, dims, preferred_element_type=F32)


def kernel(pair, mask_smem, mask_vmem, gains, biases, w_in, w_out, out,
           x, normed, gate, w_t, cols, send, recv0, recv1, back, ret0, ret1,
           stage, m_left, m_right, wide,
           send_sems, recv_sems, back_sems, ret_sems):
    r, q = lax.axis_index("row"), lax.axis_index("col")
    me = r * NC + q

    barrier = pltpu.get_barrier_semaphore()

    def greet(o, carry):
        peer = me ^ o
        pl.semaphore_signal(barrier, inc=1, device_id=(peer // NC, peer % NC), device_id_type=MESH)
        return carry

    lax.fori_loop(1, ND, greet, 0)

    for l in range(2):
        w_t[l] = w_in[l, :, : 4 * C].T
        cols[l, 0] = jnp.broadcast_to(gains[2 * l + 1 : 2 * l + 2, :], (C, C)).T
        cols[l, 1] = jnp.broadcast_to(biases[2 * l + 1 : 2 * l + 2, :], (C, C)).T

    low = lax.broadcasted_iota(jnp.int32, (1, C), 1) < ROWS
    pair_rows = mask_vmem[pl.ds(r // 2, 1), :].astype(F32)
    turned = pltpu.roll(pair_rows, ROWS, 1)
    mine = jnp.where(r % 2 == 0, pair_rows, turned)
    row_mask = jnp.where(low, mine, pltpu.roll(mine, ROWS, 1))

    def chunk_mask(s):
        a = mask_smem[q * COLS + s].astype(F32)
        b = mask_smem[q * COLS + CHUNKS + s].astype(F32)
        return row_mask * jnp.where(low, a, b)

    def project(l, t, source):
        mean = jnp.mean(source, axis=-1, keepdims=True)
        centred = source - mean
        var = jnp.mean(centred * centred, axis=-1, keepdims=True)
        g, b = gains[2 * l : 2 * l + 1, :], biases[2 * l : 2 * l + 1, :]
        n = (centred * lax.rsqrt(var + 1e-05) * g + b).astype(BF16)
        normed[pl.ds(t * 256, 256), :] = n
        mask = jnp.concatenate([chunk_mask(2 * t), chunk_mask(2 * t + 1)], axis=1)
        for side in range(2):
            value = dot(w_t[l, side * C : (side + 1) * C, :], n, NT)
            gated = dot(w_t[l, (side + 2) * C : (side + 3) * C, :], n, NT)
            res = value * jax.nn.sigmoid(gated) * mask
            for e in range(2):
                wide[pl.ds(side * 16 + 2 * t + e, C, stride=32), :] = res[:, e * C : (e + 1) * C]

    def send_out(recv, send_sem, recv_sem):
        def group(g, carry):
            base = pl.multiple_of((me ^ (g * 8)) // 8 * 8, 8)
            send[pl.ds(base, 8)] = wide[pl.ds(base * 32, 256), :].astype(BF16).reshape(8, 32, C)

            def one(j, carry):
                peer = me ^ (g * 8 + j)

                @pl.when(peer != me)
                def _():
                    pltpu.make_async_remote_copy(
                        src_ref=send.at[peer], dst_ref=recv.at[me], send_sem=send_sem, recv_sem=recv_sem,
                        device_id=(peer // NC, peer % NC), device_id_type=MESH).start()
                return carry

            return lax.fori_loop(0, 8, one, carry)

        lax.fori_loop(0, ND // 8, group, 0)
        recv[me] = send[me]

    def gates(l):
        def one(t, carry):
            rows = pl.ds(pl.multiple_of(t * 256, 256), 256)
            gate[rows, :] = jax.nn.sigmoid(dot(normed[rows, :], w_in[l, :, 4 * C :], NN))
            return carry
        lax.fori_loop(0, 8, one, 0)

    def wait_all(ref, sem):
        part = ref.at[pl.ds(0, ND - 1)]
        pltpu.make_async_copy(part, part, sem).wait()

    def combine(l, recv, ret, back_sem, ret_sem):
        for rp in range(4):
            def assemble(qq, carry):
                t0 = recv[(2 * rp) * NC + qq].astype(F32)
                t1 = recv[(2 * rp + 1) * NC + qq].astype(F32)
                a = jnp.where(low, t0, pltpu.roll(t1, ROWS, 1)).astype(BF16)
                b = jnp.where(low, pltpu.roll(t0, ROWS, 1), t1).astype(BF16)
                lanes = pl.ds(rp * C, C)
                m_left[qq, 0:16, lanes] = a[0:16]
                m_left[qq, 16:32, lanes] = b[0:16]
                m_right[qq, 0:16, lanes] = a[16:32]
                m_right[qq, 16:32, lanes] = b[16:32]
                return carry
            lax.fori_loop(0, NC, assemble, 0)
        left = m_left[...].reshape(512, 512)
        for qb in range(4):
            if l == 0:
                right = m_right[:, :, qb * C : (qb + 1) * C].reshape(512, C)
                res = dot(right, left, TN)
            else:
                right = m_right[qb * 4 : (qb + 1) * 4].reshape(C, 512)
                res = dot(right, left, NT)
            for qi in range(4):
                for rp in range(4):
                    lanes = slice(rp * C, (rp + 1) * C)
                    x0 = res[qi * 32 : qi * 32 + 16, lanes]
                    x1 = res[qi * 32 + 16 : qi * 32 + 32, lanes]
                    back[2 * rp * NC + qb * 4 + qi] = jnp.where(low, x0, pltpu.roll(x1, ROWS, 1)).astype(BF16)
                    back[(2 * rp + 1) * NC + qb * 4 + qi] = jnp.where(low, pltpu.roll(x0, ROWS, 1), x1).astype(BF16)

        def one(o, carry):
            peer = me ^ o
            pltpu.make_async_remote_copy(
                src_ref=back.at[peer], dst_ref=ret.at[me], send_sem=back_sem, recv_sem=ret_sem,
                device_id=(peer // NC, peer % NC), device_id_type=MESH).start()
            return carry

        lax.fori_loop(1, ND, one, 0)
        ret[me] = back[me]

    def finish(l, t):
        parts = []
        for e in range(2):
            v = stage[pl.ds(2 * t + e, C, stride=16), :]
            mean = jnp.mean(v, axis=0, keepdims=True)
            centred = v - mean
            var = jnp.mean(centred * centred, axis=0, keepdims=True)
            n = (centred * lax.rsqrt(var + 1e-05) * cols[l, 0] + cols[l, 1]).astype(BF16)
            parts.append(dot(n, w_out[l], TN))
        rows = pl.ds(pl.multiple_of(t * 256, 256), 256)
        return x[rows, :] + gate[rows, :] * jnp.concatenate(parts, axis=0)

    def unstage(ret):
        def one(t, carry):
            stage[pl.ds(t * 256, 256), :] = ret[pl.ds(t * 16, 16)].astype(F32).reshape(256, C)
            return carry
        lax.fori_loop(0, 8, one, 0)

    def first(t, carry):
        pieces = [pair[pl.ds(h * 16 + 2 * t + e, ROWS, stride=COLS), :] for e in range(2) for h in range(2)]
        source = jnp.concatenate(pieces, axis=0)
        x[pl.ds(pl.multiple_of(t * 256, 256), 256), :] = source
        project(0, t, source)
        return carry

    lax.fori_loop(0, 8, first, 0)
    pl.semaphore_wait(barrier, ND - 1)
    send_out(recv0, send_sems.at[0], recv_sems.at[0])
    gates(0)
    wait_all(recv0, recv_sems.at[0])
    combine(0, recv0, ret0, back_sems.at[0], ret_sems.at[0])
    wait_all(ret0, ret_sems.at[0])
    wait_all(send, send_sems.at[0])
    wait_all(back, back_sems.at[0])
    unstage(ret0)

    def second(t, carry):
        source = finish(0, t)
        x[pl.ds(pl.multiple_of(t * 256, 256), 256), :] = source
        project(1, t, source)
        return carry

    lax.fori_loop(0, 8, second, 0)
    send_out(recv1, send_sems.at[1], recv_sems.at[1])
    gates(1)
    wait_all(recv1, recv_sems.at[1])
    combine(1, recv1, ret1, back_sems.at[1], ret_sems.at[1])
    wait_all(ret1, ret_sems.at[1])
    wait_all(send, send_sems.at[1])
    wait_all(back, back_sems.at[1])
    unstage(ret1)

    def third(t, carry):
        res = finish(1, t)
        for e in range(2):
            for h in range(2):
                at = (2 * e + h) * ROWS
                out[pl.ds(h * 16 + 2 * t + e, ROWS, stride=COLS), :] = res[at : at + ROWS]
        return carry

    lax.fori_loop(0, 8, third, 0)


def body(pair, token_mask, norm_gains, norm_biases, in_weights, out_weights):
    vmem = pl.BlockSpec(memory_space=pltpu.VMEM)
    res = pl.pallas_call(
        kernel,
        out_shape=jax.ShapeDtypeStruct((ROWS * COLS, C), F32),
        in_specs=[vmem, pl.BlockSpec(memory_space=pltpu.SMEM)] + [vmem] * 5,
        out_specs=vmem,
        scratch_shapes=[
            pltpu.VMEM((2048, C), F32),
            pltpu.VMEM((2048, C), BF16),
            pltpu.VMEM((2048, C), F32),
            pltpu.VMEM((2, 4 * C, C), BF16),
            pltpu.VMEM((2, 2, C, C), F32),
            pltpu.VMEM((ND, 32, C), BF16),
            pltpu.VMEM((ND, 32, C), BF16),
            pltpu.VMEM((ND, 32, C), BF16),
            pltpu.VMEM((ND, 16, C), BF16),
            pltpu.VMEM((ND, 16, C), BF16),
            pltpu.VMEM((ND, 16, C), BF16),
            pltpu.VMEM((2048, C), F32),
            pltpu.VMEM((NC, 32, 512), BF16),
            pltpu.VMEM((NC, 32, 512), BF16),
            pltpu.VMEM((4096, C), F32),
            pltpu.SemaphoreType.DMA((2,)),
            pltpu.SemaphoreType.DMA((2,)),
            pltpu.SemaphoreType.DMA((2,)),
            pltpu.SemaphoreType.DMA((2,)),
        ],
        compiler_params=pltpu.CompilerParams(
            collective_id=0, has_side_effects=True, vmem_limit_bytes=48 << 20),
    )(
        pair.reshape(ROWS * COLS, C), token_mask, token_mask.reshape(4, C),
        norm_gains.reshape(4, C), norm_biases.reshape(4, C), in_weights, out_weights,
    )
    return res.reshape(ROWS, COLS, C)


def solution(mesh):
    placed = (P("row", "col", None), P(), P(), P(), P(), P())
    return jax.shard_map(
        body, mesh=mesh, in_specs=placed, out_specs=P("row", "col", None), check_vma=False
    )
```

```python
import jax
import jax.numpy as jnp
from jax import lax
from jax.experimental import pallas as pl
from jax.experimental.pallas import tpu as pltpu
from jax.sharding import PartitionSpec as P

MESH = pl.DeviceIdType.MESH
F32, BF16 = jnp.float32, jnp.bfloat16
C = 128
ROWS, COLS = 64, 32
NR, NC = 8, 16
ND = NR * NC
CHUNKS = 16
GROUPS = 4
MEMBERS = ND // GROUPS
TN = (((0,), (0,)), ((), ()))
NT = (((1,), (1,)), ((), ()))
NN = (((1,), (0,)), ((), ()))


def dot(a, b, dims):
    return lax.dot_general(a, b, dims, preferred_element_type=F32)


def place(device):
    return (device // NC, device % NC)


def group_offset(g, k):
    k = (7 * k) % MEMBERS
    return (g // 2) * 64 + (g % 2) * 16 + (k // 16) * 32 + k % 16


def kernel(pair_hbm, mask_smem, mask_vmem, gains, biases, w_in_hbm, w_out_hbm, out,
           pair, w_in, w_out, x, normed, gate, w_t, cols, send, recv0, recv1, back, ret0, ret1,
           stage, m_left, m_right, wide,
           load_sems, send_sems, recv_sems, back_sems, ret_sems):
    r, q = lax.axis_index("row"), lax.axis_index("col")
    me = r * NC + q

    barrier = pltpu.get_barrier_semaphore()

    def greet(i, carry):
        i = ND - 1 - i
        hi, lo = i // 16, 15 - i % 16
        o = (hi // 4) * 32 + (hi // 2 % 2) * 8 + (hi % 2) * 4
        o = o + (lo // 8) * 64 + (lo // 4 % 2) * 16 + lo % 4

        @pl.when(o != 0)
        def _():
            pl.semaphore_signal(barrier, inc=1, device_id=place(me ^ o), device_id_type=MESH)
        return carry

    loads = [
        pltpu.make_async_copy(w_in_hbm, w_in, load_sems.at[0]),
        pltpu.make_async_copy(pair_hbm, pair, load_sems.at[1]),
        pltpu.make_async_copy(w_out_hbm, w_out, load_sems.at[2]),
    ]
    for load in loads:
        load.start()
    lax.fori_loop(0, ND, greet, 0)

    low = lax.broadcasted_iota(jnp.int32, (1, C), 1) < ROWS
    pair_rows = mask_vmem[pl.ds(r // 2, 1), :].astype(F32)
    turned = pltpu.roll(pair_rows, ROWS, 1)
    mine = jnp.where(r % 2 == 0, pair_rows, turned)
    row_mask = jnp.where(low, mine, pltpu.roll(mine, ROWS, 1))

    def chunk_mask(s):
        a = mask_smem[q * COLS + s].astype(F32)
        b = mask_smem[q * COLS + CHUNKS + s].astype(F32)
        return row_mask * jnp.where(low, a, b)

    for l in range(2):
        cols[l, 0] = jnp.broadcast_to(gains[2 * l + 1 : 2 * l + 2, :], (C, C)).T
        cols[l, 1] = jnp.broadcast_to(biases[2 * l + 1 : 2 * l + 2, :], (C, C)).T
    loads[0].wait()
    for l in range(2):
        w_t[l] = w_in[l, :, : 4 * C].T
    loads[1].wait()
    loads[2].wait()

    def project(l, t, source):
        mean = jnp.mean(source, axis=-1, keepdims=True)
        centred = source - mean
        var = jnp.mean(centred * centred, axis=-1, keepdims=True)
        g, b = gains[2 * l : 2 * l + 1, :], biases[2 * l : 2 * l + 1, :]
        n = (centred * lax.rsqrt(var + 1e-05) * g + b).astype(BF16)
        normed[pl.ds(t * 256, 256), :] = n
        mask = jnp.concatenate([chunk_mask(2 * t), chunk_mask(2 * t + 1)], axis=1)
        for side in range(2):
            value = dot(w_t[l, side * C : (side + 1) * C, :], n, NT)
            gated = dot(w_t[l, (side + 2) * C : (side + 3) * C, :], n, NT)
            res = value * jax.nn.sigmoid(gated) * mask
            for e in range(2):
                wide[pl.ds(side * 16 + 2 * t + e, C, stride=32), :] = res[:, e * C : (e + 1) * C]

    def pack_send():
        def one(g, carry):
            send[pl.ds(g * 8, 8)] = wide[pl.ds(g * 256, 256), :].astype(BF16).reshape(8, 32, C)
            return carry

        lax.fori_loop(0, ND // 8, one, 0, unroll=4)

    def send_out(l, recv):
        for g in range(GROUPS):
            def one(k, carry):
                peer = me ^ group_offset(g, k)
                pltpu.make_async_remote_copy(
                    src_ref=send.at[peer], dst_ref=recv.at[me],
                    send_sem=send_sems.at[l], recv_sem=recv_sems.at[l, g],
                    device_id=place(peer), device_id_type=MESH).start()
                return carry

            lax.fori_loop(1 if g == 0 else 0, MEMBERS, one, 0)
        recv[me] = send[me]

    def gates(l):
        def one(t, carry):
            rows = pl.ds(pl.multiple_of(t * 256, 256), 256)
            gate[rows, :] = jax.nn.sigmoid(dot(normed[rows, :], w_in[l, :, 4 * C :], NN))
            return carry
        lax.fori_loop(0, 8, one, 0, unroll=4)

    def wait_for(ref, count, sem):
        part = ref.at[pl.ds(0, count)]
        pltpu.make_async_copy(part, part, sem).wait()

    def combine(l, recv, ret):
        for g in range(GROUPS):
            wait_for(recv, MEMBERS - (g == 0), recv_sems.at[l, g])
            ra = (r ^ ((g // 2) * 4 + g % 2)) // 4 * 4 + (r ^ g) % 2
            for c in range(NC):
                t0 = recv[ra * NC + c].astype(F32)
                t1 = recv[(ra + 2) * NC + c].astype(F32)
                a = jnp.where(low, t0, pltpu.roll(t1, ROWS, 1)).astype(BF16)
                b = jnp.where(low, pltpu.roll(t0, ROWS, 1), t1).astype(BF16)
                lanes = slice(g * C, (g + 1) * C)
                m_left[c, 0:16, lanes] = a[0:16]
                m_left[c, 16:32, lanes] = b[0:16]
                m_right[c, 0:16, lanes] = a[16:32]
                m_right[c, 16:32, lanes] = b[16:32]
        left = m_left[...].reshape(512, 512)
        for step in range(4):
            if l == 0:
                a0, a1 = (q // 8 + step % 2) % 2, (q // 2 + step // 2) % 2
                rel = (a0 + r // 4) % 2 * 2 + (a1 + r) % 2
                right = m_right[:, :, pl.ds(pl.multiple_of(rel * C, C), C)].reshape(512, C)
                res = dot(right, left, TN)
                targets = [2 * (a0 * 4 + jh * 2 + a1) + jq for jh in range(2) for jq in range(2)]
            else:
                b = (q % 4) ^ step
                right = jnp.concatenate([m_right[b + 4 * m] for m in range(4)], axis=0)
                res = dot(right, left, NT)
                targets = [b + 4 * m for m in range(4)]
            for i, tq in enumerate(targets):
                for g in range(4):
                    if l == 0:
                        ra = (r ^ ((g // 2) * 4 + g % 2)) // 4 * 4 + (r ^ g) % 2
                        rb = ra + 2
                    else:
                        ra, rb = 2 * g, 2 * g + 1
                    x0 = res[i * 32 : i * 32 + 16, g * C : (g + 1) * C]
                    x1 = res[i * 32 + 16 : i * 32 + 32, g * C : (g + 1) * C]
                    back[ra * NC + tq] = jnp.where(low, x0, pltpu.roll(x1, ROWS, 1)).astype(BF16)
                    back[rb * NC + tq] = jnp.where(low, pltpu.roll(x0, ROWS, 1), x1).astype(BF16)

            def one(k, carry):
                k = (7 * k) % MEMBERS
                tr = r ^ (k % 8)
                kq = k // 8
                if l == 0:
                    tq = (a0 * 8 + a1 * 2) + (q ^ (kq // 2 * 4 + kq % 2)) % 8 // 4 * 4 + (q ^ kq) % 2
                else:
                    tq = (q ^ (kq * 4)) // 4 * 4 + b
                peer = tr * NC + tq

                @pl.when(peer != me)
                def _():
                    pltpu.make_async_remote_copy(
                        src_ref=back.at[peer], dst_ref=ret.at[me],
                        send_sem=back_sems.at[l], recv_sem=ret_sems.at[l],
                        device_id=place(peer), device_id_type=MESH).start()
                return carry

            lax.fori_loop(0, MEMBERS, one, 0)
        ret[me] = back[me]

    def finish(l, t):
        parts = []
        for e in range(2):
            v = stage[pl.ds(2 * t + e, C, stride=16), :]
            mean = jnp.mean(v, axis=0, keepdims=True)
            centred = v - mean
            var = jnp.mean(centred * centred, axis=0, keepdims=True)
            n = (centred * lax.rsqrt(var + 1e-05) * cols[l, 0] + cols[l, 1]).astype(BF16)
            parts.append(dot(n, w_out[l], TN))
        rows = pl.ds(pl.multiple_of(t * 256, 256), 256)
        return x[rows, :] + gate[rows, :] * jnp.concatenate(parts, axis=0)

    def receive(l, ret):
        wait_for(ret, ND - 1, ret_sems.at[l])
        wait_for(send, ND - 1, send_sems.at[l])
        wait_for(back, ND - 1, back_sems.at[l])

        def one(t, carry):
            stage[pl.ds(t * 256, 256), :] = ret[pl.ds(t * 16, 16)].astype(F32).reshape(256, C)
            return carry
        lax.fori_loop(0, 8, one, 0, unroll=4)

    def first(t, carry):
        pieces = [pair[pl.ds(h * 16 + 2 * t + e, ROWS, stride=COLS), :] for e in range(2) for h in range(2)]
        source = jnp.concatenate(pieces, axis=0)
        x[pl.ds(pl.multiple_of(t * 256, 256), 256), :] = source
        project(0, t, source)
        return carry

    lax.fori_loop(0, 8, first, 0, unroll=4)
    pack_send()
    gates(0)
    pl.semaphore_wait(barrier, ND - 1)
    send_out(0, recv0)
    combine(0, recv0, ret0)
    receive(0, ret0)

    def second(t, carry):
        source = finish(0, t)
        x[pl.ds(pl.multiple_of(t * 256, 256), 256), :] = source
        project(1, t, source)
        return carry

    lax.fori_loop(0, 8, second, 0, unroll=4)
    pack_send()
    send_out(1, recv1)
    gates(1)
    combine(1, recv1, ret1)
    receive(1, ret1)

    def third(t, carry):
        res = finish(1, t)
        for e in range(2):
            for h in range(2):
                at = (2 * e + h) * ROWS
                out[pl.ds(h * 16 + 2 * t + e, ROWS, stride=COLS), :] = res[at : at + ROWS]
        return carry

    lax.fori_loop(0, 8, third, 0, unroll=4)


def body(pair, token_mask, norm_gains, norm_biases, in_weights, out_weights):
    vmem = pl.BlockSpec(memory_space=pltpu.VMEM)
    hbm = pl.BlockSpec(memory_space=pltpu.HBM)
    res = pl.pallas_call(
        kernel,
        out_shape=jax.ShapeDtypeStruct((ROWS * COLS, C), F32),
        in_specs=[hbm, pl.BlockSpec(memory_space=pltpu.SMEM), vmem, vmem, vmem, hbm, hbm],
        out_specs=vmem,
        scratch_shapes=[
            pltpu.VMEM((2048, C), F32),
            pltpu.VMEM((2, C, 5 * C), BF16),
            pltpu.VMEM((2, C, C), BF16),
            pltpu.VMEM((2048, C), F32),
            pltpu.VMEM((2048, C), BF16),
            pltpu.VMEM((2048, C), F32),
            pltpu.VMEM((2, 4 * C, C), BF16),
            pltpu.VMEM((2, 2, C, C), F32),
            pltpu.VMEM((ND, 32, C), BF16),
            pltpu.VMEM((ND, 32, C), BF16),
            pltpu.VMEM((ND, 32, C), BF16),
            pltpu.VMEM((ND, 16, C), BF16),
            pltpu.VMEM((ND, 16, C), BF16),
            pltpu.VMEM((ND, 16, C), BF16),
            pltpu.VMEM((2048, C), F32),
            pltpu.VMEM((NC, 32, 512), BF16),
            pltpu.VMEM((NC, 32, 512), BF16),
            pltpu.VMEM((4096, C), F32),
            pltpu.SemaphoreType.DMA((3,)),
            pltpu.SemaphoreType.DMA((2,)),
            pltpu.SemaphoreType.DMA((2, GROUPS)),
            pltpu.SemaphoreType.DMA((2,)),
            pltpu.SemaphoreType.DMA((2,)),
        ],
        compiler_params=pltpu.CompilerParams(
            collective_id=0, has_side_effects=True, vmem_limit_bytes=48 << 20),
    )(
        pair.reshape(ROWS * COLS, C), token_mask, token_mask.reshape(4, C),
        norm_gains.reshape(4, C), norm_biases.reshape(4, C), in_weights, out_weights,
    )
    return res.reshape(ROWS, COLS, C)


def solution(mesh):
    placed = (P("row", "col", None), P(), P(), P(), P(), P())
    return jax.shard_map(
        body, mesh=mesh, in_specs=placed, out_specs=P("row", "col", None), check_vma=False
    )
```

```python
import jax
import jax.numpy as jnp
from jax import lax
from jax.experimental import pallas as pl
from jax.experimental.pallas import tpu as pltpu
from jax.sharding import PartitionSpec as P

MESH = pl.DeviceIdType.MESH
F32, BF16 = jnp.float32, jnp.bfloat16
C = 128
ROWS, COLS = 64, 32
NR, NC = 8, 16
ND = NR * NC
CHUNKS = 16
GROUPS = 4
MEMBERS = ND // GROUPS
TN = (((0,), (0,)), ((), ()))
NT = (((1,), (1,)), ((), ()))
NN = (((1,), (0,)), ((), ()))


def dot(a, b, dims):
    return lax.dot_general(a, b, dims, preferred_element_type=F32)


def place(device):
    return (device >> 4, device & 15)


def group_offset(g, k):
    k = (7 * k) % MEMBERS
    return (g // 2) * 64 + (g % 2) * 16 + (k // 16) * 32 + k % 16


def norm_rows(v, gain, bias):
    mean = jnp.mean(v, axis=0, keepdims=True)
    centred = v - mean
    var = jnp.mean(centred * centred, axis=0, keepdims=True)
    return (centred * lax.rsqrt(var + 1e-05) * gain + bias).astype(BF16)


def kernel(pair_hbm, mask_smem, mask_vmem, gains, biases, w_in_hbm, w_out_hbm, out,
           pair, w_in, w_out, x, x_pos, normed, gate, w_t, w_gate_t, w_out_t, mask, cols,
           send, recv0, recv1, back, ret0, ret1, stage, m_left, m_right, wide,
           load_sems, in_sems, send_sems, recv_sems, back_sems, ret_sems):
    r, q = lax.axis_index("row"), lax.axis_index("col")
    me = r * NC + q
    quarter = (r >> 2) * 2 + (r & 1)

    barrier = pltpu.get_barrier_semaphore()
    loads = [
        pltpu.make_async_copy(w_in_hbm, w_in, load_sems.at[0]),
        pltpu.make_async_copy(pair_hbm, pair, load_sems.at[1]),
        pltpu.make_async_copy(w_out_hbm, w_out, load_sems.at[2]),
    ]
    for load in loads:
        load.start()
    for o in [group_offset(0, k) for k in range(1, MEMBERS)] + [group_offset(g, 0) for g in range(1, GROUPS)]:
        pl.semaphore_signal(barrier, inc=1, device_id=place(me ^ o), device_id_type=MESH)

    low = lax.broadcasted_iota(jnp.int32, (1, C), 1) < ROWS
    pair_rows = mask_vmem[pl.ds(r >> 1, 1), :].astype(F32)
    turned = pltpu.roll(pair_rows, ROWS, 1)
    mine = jnp.where((r & 1) == 0, pair_rows, turned)
    row_mask = jnp.where(low, mine, pltpu.roll(mine, ROWS, 1))
    for s in range(CHUNKS):
        a = mask_smem[q * COLS + s].astype(F32)
        b = mask_smem[q * COLS + CHUNKS + s].astype(F32)
        mask[s // 2, :, (s % 2) * C : (s % 2 + 1) * C] = row_mask * jnp.where(low, a, b)

    for l in range(2):
        for i in range(2):
            cols[l, i, 0] = jnp.broadcast_to(gains[2 * l + i : 2 * l + i + 1, :], (C, C)).T
            cols[l, i, 1] = jnp.broadcast_to(biases[2 * l + i : 2 * l + i + 1, :], (C, C)).T

    def turn_weights(l):
        for part in range(4):
            t = w_in[l, :, part * C : (part + 1) * C].T
            for d in range(8):
                at = part * 32 + (d // 2 % 2) * 16
                w_t[l, (d // 4) * 2 + d % 2, at : at + 16, :] = t[d * 16 : (d + 1) * 16, :]

    def first(t):
        for e in range(2):
            s = 2 * t + e
            pieces = [pair[pl.ds(h * 16 + s, ROWS, stride=COLS), :] for h in range(2)]
            v = jnp.concatenate(pieces, axis=0).T
            x[s] = v
            normed[:, s * C : (s + 1) * C] = norm_rows(v, cols[0, 0, 0], cols[0, 0, 1])

    def project(l, g):
        part = quarter ^ g
        w = w_t[l, part]
        base = (g % 2) * 1024
        for t in range(8):
            res = dot(w, normed[:, t * 256 : (t + 1) * 256], NN)
            for side in range(2):
                value = res[side * 32 : (side + 1) * 32]
                gated = res[64 + side * 32 : 64 + (side + 1) * 32]
                both = value * jax.nn.sigmoid(gated) * mask[t]
                for e in range(2):
                    wide[pl.ds(base + side * 16 + 2 * t + e, 32, stride=32), :] = both[:, e * C : (e + 1) * C]
        for i in range(4):
            at = (part >> 1) * 64 + (part & 1) * 16 + (i // 2) * 32 + (i % 2) * 8
            rows = wide[base + i * 256 : base + (i + 1) * 256, :]
            send[pl.ds(at, 8)] = rows.astype(BF16).reshape(8, 32, C)

    def send_group(l, g, recv):
        for k in range(1 if g == 0 else 0, MEMBERS):
            peer = me ^ group_offset(g, k)
            pltpu.make_async_remote_copy(
                src_ref=send.at[peer], dst_ref=recv.at[me],
                send_sem=send_sems.at[l], recv_sem=recv_sems.at[l, g],
                device_id=place(peer), device_id_type=MESH).start()
        if g == 0:
            recv[me] = send[me]

    def wait_for(ref, count, sem):
        part = ref.at[pl.ds(0, count)]
        pltpu.make_async_copy(part, part, sem).wait()

    def rows_of(g):
        ra = (r ^ ((g // 2) * 4 + g % 2)) & 5
        return ra, ra + 2

    def combine(l, recv, ret):
        for g in range(GROUPS):
            wait_for(recv, MEMBERS - (g == 0), recv_sems.at[l, g])
            ra, rb = rows_of(g)
            for c in range(NC):
                t0 = recv[ra * NC + c].astype(F32)
                t1 = recv[rb * NC + c].astype(F32)
                a = jnp.where(low, t0, pltpu.roll(t1, ROWS, 1)).astype(BF16)
                b = jnp.where(low, pltpu.roll(t0, ROWS, 1), t1).astype(BF16)
                lanes = slice(g * C, (g + 1) * C)
                m_left[c, 0:16, lanes] = a[0:16]
                m_left[c, 16:32, lanes] = b[0:16]
                m_right[c, 0:16, lanes] = a[16:32]
                m_right[c, 16:32, lanes] = b[16:32]
        left = m_left[...].reshape(512, 512)
        for step in range(4):
            if l == 0:
                a0, a1 = (q >> 3) ^ (step % 2), ((q >> 1) & 1) ^ (step // 2)
                rel = (a0 ^ (r >> 2)) * 2 + (a1 ^ (r & 1))
                right = m_right[:, :, pl.ds(pl.multiple_of(rel * C, C), C)].reshape(512, C)
                res = dot(right, left, TN)
                targets = [a0 * 8 + jh * 4 + a1 * 2 + jq for jh in range(2) for jq in range(2)]
            else:
                b = (q & 3) ^ step
                right = jnp.concatenate([m_right[b + 4 * m] for m in range(4)], axis=0)
                res = dot(right, left, NT)
                targets = [b + 4 * m for m in range(4)]
            for i, tq in enumerate(targets):
                for g in range(4):
                    ra, rb = rows_of(g) if l == 0 else (2 * g, 2 * g + 1)
                    x0 = res[i * 32 : i * 32 + 16, g * C : (g + 1) * C]
                    x1 = res[i * 32 + 16 : i * 32 + 32, g * C : (g + 1) * C]
                    back[ra * NC + tq] = jnp.where(low, x0, pltpu.roll(x1, ROWS, 1)).astype(BF16)
                    back[rb * NC + tq] = jnp.where(low, pltpu.roll(x0, ROWS, 1), x1).astype(BF16)
            for k in range(MEMBERS):
                k = (7 * k) % MEMBERS
                kq = k // 8
                if l == 0:
                    o = (step % 2) * 8 + (step // 2) * 2 + (kq // 2) * 4 + kq % 2
                else:
                    o = kq * 4 + step
                o += (k % 8) * NC
                if o == 0:
                    continue
                peer = me ^ o
                pltpu.make_async_remote_copy(
                    src_ref=back.at[peer], dst_ref=ret.at[me],
                    send_sem=back_sems.at[l], recv_sem=ret_sems.at[l],
                    device_id=place(peer), device_id_type=MESH).start()
        ret[me] = back[me]

    def receive(l, ret):
        wait_for(ret, ND - 1, ret_sems.at[l])
        for t in range(8):
            stage[t * 256 : (t + 1) * 256, :] = ret[t * 16 : (t + 1) * 16].astype(F32).reshape(256, C)

    def normed_out(l, s):
        return norm_rows(stage[pl.ds(s, C, stride=16), :], cols[l, 1, 0], cols[l, 1, 1])

    loads[0].wait()
    turn_weights(0)
    loads[1].wait()
    for t in range(8):
        first(t)
    project(0, 0)
    pl.semaphore_wait(barrier, MEMBERS - 1 + GROUPS - 1)
    for g in range(1, GROUPS):
        pl.semaphore_signal(in_sems.at[g], inc=1, device_id=place(me ^ group_offset(g, 0)), device_id_type=MESH)
    send_group(0, 0, recv0)
    for g in range(1, GROUPS):
        project(0, g)
        pl.semaphore_wait(in_sems.at[g], 1)
        send_group(0, g, recv0)
    loads[2].wait()
    for l in range(2):
        w_out_t[l] = w_out[l].T
    w_gate_t[...] = w_in[0, :, 4 * C :].T
    for t in range(CHUNKS):
        gate[t] = jax.nn.sigmoid(dot(w_gate_t[...], normed[:, t * C : (t + 1) * C], NN))
    turn_weights(1)
    combine(0, recv0, ret0)
    wait_for(send, ND - 1, send_sems.at[0])
    receive(0, ret0)

    for s in range(CHUNKS):
        v = x[s] + gate[s] * dot(w_out_t[0], normed_out(0, s), NN)
        x[s] = v
        normed[:, s * C : (s + 1) * C] = norm_rows(v, cols[1, 0, 0], cols[1, 0, 1])
    for g in range(GROUPS):
        project(1, g)
        send_group(1, g, recv1)
    for s in range(CHUNKS):
        x_pos[s] = x[s].T
        gate[s] = jax.nn.sigmoid(dot(normed[:, s * C : (s + 1) * C], w_in[1, :, 4 * C :], TN))
    wait_for(back, ND - 1, back_sems.at[0])
    combine(1, recv1, ret1)
    wait_for(send, ND - 1, send_sems.at[1])
    receive(1, ret1)
    wait_for(back, ND - 1, back_sems.at[1])

    for s in range(CHUNKS):
        res = x_pos[s] + gate[s] * dot(normed_out(1, s), w_out[1], TN)
        for h in range(2):
            out[pl.ds(h * 16 + s, ROWS, stride=COLS), :] = res[h * ROWS : (h + 1) * ROWS]


def body(pair, token_mask, norm_gains, norm_biases, in_weights, out_weights):
    vmem = pl.BlockSpec(memory_space=pltpu.VMEM)
    hbm = pl.BlockSpec(memory_space=pltpu.HBM)
    res = pl.pallas_call(
        kernel,
        out_shape=jax.ShapeDtypeStruct((ROWS * COLS, C), F32),
        in_specs=[hbm, pl.BlockSpec(memory_space=pltpu.SMEM), vmem, vmem, vmem, hbm, hbm],
        out_specs=vmem,
        scratch_shapes=[
            pltpu.VMEM((2048, C), F32),
            pltpu.VMEM((2, C, 5 * C), BF16),
            pltpu.VMEM((2, C, C), BF16),
            pltpu.VMEM((CHUNKS, C, C), F32),
            pltpu.VMEM((CHUNKS, C, C), F32),
            pltpu.VMEM((C, 2048), BF16),
            pltpu.VMEM((CHUNKS, C, C), F32),
            pltpu.VMEM((2, GROUPS, C, C), BF16),
            pltpu.VMEM((C, C), BF16),
            pltpu.VMEM((2, C, C), BF16),
            pltpu.VMEM((8, 1, 256), F32),
            pltpu.VMEM((2, 2, 2, C, C), F32),
            pltpu.VMEM((ND, 32, C), BF16),
            pltpu.VMEM((ND, 32, C), BF16),
            pltpu.VMEM((ND, 32, C), BF16),
            pltpu.VMEM((ND, 16, C), BF16),
            pltpu.VMEM((ND, 16, C), BF16),
            pltpu.VMEM((ND, 16, C), BF16),
            pltpu.VMEM((2048, C), F32),
            pltpu.VMEM((NC, 32, 512), BF16),
            pltpu.VMEM((NC, 32, 512), BF16),
            pltpu.VMEM((2048, C), F32),
            pltpu.SemaphoreType.DMA((3,)),
            pltpu.SemaphoreType.REGULAR((GROUPS,)),
            pltpu.SemaphoreType.DMA((2,)),
            pltpu.SemaphoreType.DMA((2, GROUPS)),
            pltpu.SemaphoreType.DMA((2,)),
            pltpu.SemaphoreType.DMA((2,)),
        ],
        compiler_params=pltpu.CompilerParams(
            collective_id=0, has_side_effects=True, vmem_limit_bytes=48 << 20),
    )(
        pair.reshape(ROWS * COLS, C), token_mask, token_mask.reshape(4, C),
        norm_gains.reshape(4, C), norm_biases.reshape(4, C), in_weights, out_weights,
    )
    return res.reshape(ROWS, COLS, C)


def solution(mesh):
    placed = (P("row", "col", None), P(), P(), P(), P(), P())
    return jax.shard_map(
        body, mesh=mesh, in_specs=placed, out_specs=P("row", "col", None), check_vma=False
    )
```

```python
import jax
import jax.numpy as jnp
from jax import lax
from jax.experimental import pallas as pl
from jax.experimental.pallas import tpu as pltpu
from jax.sharding import PartitionSpec as P

MESH = pl.DeviceIdType.MESH
F32, BF16 = jnp.float32, jnp.bfloat16
C = 128
ROWS, COLS = 64, 32
NR, NC = 8, 16
ND = NR * NC
CHUNKS = 16
GROUPS = 4
MEMBERS = ND // GROUPS
TN = (((0,), (0,)), ((), ()))
NT = (((1,), (1,)), ((), ()))
NN = (((1,), (0,)), ((), ()))


def dot(a, b, dims):
    return lax.dot_general(a, b, dims, preferred_element_type=F32)


def place(device):
    return (device >> 4, device & 15)


def hops(o):
    return sum((0, 1, 2, 1)[(o >> hi & 1) * 2 + (o >> lo & 1)] for hi, lo in ((3, 6), (5, 4), (2, 1)))


def group_bits(g):
    return (g // 2) * 64 + (g % 2) * 16


def far_first(offsets):
    offsets = list(offsets)
    mixed = [offsets[(7 * k) % len(offsets)] for k in range(len(offsets))]
    return sorted(mixed, key=lambda o: -hops(o))


def group_offsets(g):
    return [o for o in far_first(group_bits(g) + (k // 16) * 32 + k % 16 for k in range(MEMBERS)) if o]


def norm_rows(v, gain, bias):
    mean = jnp.mean(v, axis=0, keepdims=True)
    centred = v - mean
    var = jnp.mean(centred * centred, axis=0, keepdims=True)
    return (centred * lax.rsqrt(var + 1e-05) * gain + bias).astype(BF16)


def kernel(pair_hbm, mask_hbm, rows_hbm, gains_hbm, biases_hbm, w_in_hbm, w_out_hbm, out,
           pair, mask_smem, mask_vmem, gains, biases, w_in, w_out, x, x_pos, normed, gate, w_t, w_gate_t, w_out_t, mask, cols,
           send, recv0, recv1, back, ret0, ret1, stage, m_left, m_right, wide,
           load_sems, in_sems, send_sems, recv_sems, back_sems, ret_sems):
    r, q = lax.axis_index("row"), lax.axis_index("col")
    me = r * NC + q
    quarter = (r >> 2) * 2 + (r & 1)

    barrier = pltpu.get_barrier_semaphore()
    loads = [
        pltpu.make_async_copy(w_in_hbm, w_in, load_sems.at[0]),
        pltpu.make_async_copy(pair_hbm, pair, load_sems.at[1]),
        pltpu.make_async_copy(w_out_hbm, w_out, load_sems.at[2]),
        pltpu.make_async_copy(mask_hbm, mask_smem, load_sems.at[3]),
        pltpu.make_async_copy(rows_hbm, mask_vmem, load_sems.at[4]),
        pltpu.make_async_copy(gains_hbm, gains, load_sems.at[5]),
        pltpu.make_async_copy(biases_hbm, biases, load_sems.at[6]),
    ]
    for load in loads:
        load.start()
    for o in group_offsets(0) + [group_bits(g) for g in range(1, GROUPS)]:
        pl.semaphore_signal(barrier, inc=1, device_id=place(me ^ o), device_id_type=MESH)

    for load in loads[3:]:
        load.wait()
    low = lax.broadcasted_iota(jnp.int32, (1, C), 1) < ROWS
    pair_rows = mask_vmem[pl.ds(r >> 1, 1), :].astype(F32)
    turned = pltpu.roll(pair_rows, ROWS, 1)
    mine = jnp.where((r & 1) == 0, pair_rows, turned)
    row_mask = jnp.where(low, mine, pltpu.roll(mine, ROWS, 1))
    for s in range(CHUNKS):
        a = mask_smem[q * COLS + s].astype(F32)
        b = mask_smem[q * COLS + CHUNKS + s].astype(F32)
        mask[s // 2, :, (s % 2) * C : (s % 2 + 1) * C] = row_mask * jnp.where(low, a, b)

    for l in range(2):
        for i in range(2):
            cols[l, i, 0] = jnp.broadcast_to(gains[2 * l + i : 2 * l + i + 1, :], (C, C)).T
            cols[l, i, 1] = jnp.broadcast_to(biases[2 * l + i : 2 * l + i + 1, :], (C, C)).T

    def turn_weights(l):
        for part in range(4):
            t = w_in[l, :, part * C : (part + 1) * C].T
            for d in range(8):
                at = part * 32 + (d // 2 % 2) * 16
                w_t[l, (d // 4) * 2 + d % 2, at : at + 16, :] = t[d * 16 : (d + 1) * 16, :]

    def first(t):
        for e in range(2):
            s = 2 * t + e
            pieces = [pair[pl.ds(h * 16 + s, ROWS, stride=COLS), :] for h in range(2)]
            v = jnp.concatenate(pieces, axis=0).T
            x[s] = v
            normed[:, s * C : (s + 1) * C] = norm_rows(v, cols[0, 0, 0], cols[0, 0, 1])

    def project(l, g):
        part = quarter ^ g
        w = w_t[l, part]
        base = (g % 2) * 1024
        for t in range(8):
            res = dot(w, normed[:, t * 256 : (t + 1) * 256], NN)
            for side in range(2):
                value = res[side * 32 : (side + 1) * 32]
                gated = res[64 + side * 32 : 64 + (side + 1) * 32]
                both = value * jax.nn.sigmoid(gated) * mask[t]
                for e in range(2):
                    wide[pl.ds(base + side * 16 + 2 * t + e, 32, stride=32), :] = both[:, e * C : (e + 1) * C]
        for i in range(4):
            at = (part >> 1) * 64 + (part & 1) * 16 + (i // 2) * 32 + (i % 2) * 8
            rows = wide[base + i * 256 : base + (i + 1) * 256, :]
            send[pl.ds(at, 8)] = rows.astype(BF16).reshape(8, 32, C)

    def send_group(l, g, recv):
        for o in group_offsets(g):
            peer = me ^ o
            pltpu.make_async_remote_copy(
                src_ref=send.at[peer], dst_ref=recv.at[me],
                send_sem=send_sems.at[l], recv_sem=recv_sems.at[l, g],
                device_id=place(peer), device_id_type=MESH).start()
        if g == 0:
            recv[me] = send[me]

    def wait_for(ref, count, sem):
        part = ref.at[pl.ds(0, count)]
        pltpu.make_async_copy(part, part, sem).wait()

    def rows_of(g):
        ra = (r ^ ((g // 2) * 4 + g % 2)) & 5
        return ra, ra + 2

    def give_back(l, ret, peer):
        pltpu.make_async_remote_copy(
            src_ref=back.at[peer], dst_ref=ret.at[me],
            send_sem=back_sems.at[l], recv_sem=ret_sems.at[l],
            device_id=place(peer), device_id_type=MESH).start()

    def assemble(l, recv, g):
        wait_for(recv, MEMBERS - (g == 0), recv_sems.at[l, g])
        ra, rb = rows_of(g)
        lanes = slice(g * C, (g + 1) * C)
        for c in range(NC):
            t0 = recv[ra * NC + c].astype(F32)
            t1 = recv[rb * NC + c].astype(F32)
            a = jnp.where(low, t0, pltpu.roll(t1, ROWS, 1)).astype(BF16)
            b = jnp.where(low, pltpu.roll(t0, ROWS, 1), t1).astype(BF16)
            m_left[c, 0:16, lanes] = a[0:16]
            m_left[c, 16:32, lanes] = b[0:16]
            m_right[c, 0:16, lanes] = a[16:32]
            m_right[c, 16:32, lanes] = b[16:32]

    def pack(tile, ra, rb, tq):
        x0, x1 = tile[0:16], tile[16:32]
        back[ra * NC + tq] = jnp.where(low, x0, pltpu.roll(x1, ROWS, 1)).astype(BF16)
        back[rb * NC + tq] = jnp.where(low, pltpu.roll(x0, ROWS, 1), x1).astype(BF16)

    def combine_outgoing(recv, ret):
        for g in range(GROUPS):
            assemble(0, recv, g)
            lanes = slice(g * C, (g + 1) * C)
            right = m_right[:, :, lanes].reshape(512, C)
            res = dot(right, m_left[:, :, : (g + 1) * C].reshape(512, (g + 1) * C), TN)
            blocks = {(g, gi): res[:, gi * C : (gi + 1) * C] for gi in range(g + 1)}
            if g:
                left = m_left[:, :, lanes].reshape(512, C)
                res = dot(m_right[:, :, : g * C].reshape(512, g * C), left, TN)
                blocks.update({(gj, g): res[gj * C : (gj + 1) * C] for gj in range(g)})
            sends = []
            for (gj, gi), block in blocks.items():
                jr, (ra, rb) = rows_of(gj)[0], rows_of(gi)
                for jh in range(2):
                    for jq in range(2):
                        at = jh * 64 + jq * 32
                        pack(block[at : at + 32], ra, rb, (jr >> 2) * 8 + jh * 4 + (jr & 1) * 2 + jq)
                for zz in range(2):
                    for yy in range(2):
                        for jq in range(2):
                            away = hops(group_bits(gi) + zz * 32) + yy
                            tr = (r ^ ((gi // 2) * 4 + gi % 2)) ^ (zz * 2)
                            tq = (jr >> 2) * 8 + ((q & 4) ^ (yy * 4)) + (jr & 1) * 2 + jq
                            sends.append((away, tr * NC + tq))
            for _, peer in sorted(sends, key=lambda e: -e[0]):
                @pl.when(peer != me)
                def _(peer=peer):
                    give_back(0, ret, peer)
        ret[me] = back[me]

    def combine_incoming(recv, ret):
        for g in range(GROUPS):
            assemble(1, recv, g)
        left = m_left[...].reshape(512, 512)
        for step in range(4):
            b = (q & 3) ^ step
            right = jnp.concatenate([m_right[b + 4 * m] for m in range(4)], axis=0)
            res = dot(right, left, NT)
            for m in range(4):
                for p in range(4):
                    pack(res[m * 32 : (m + 1) * 32, p * C : (p + 1) * C], 2 * p, 2 * p + 1, b + 4 * m)
            for o in far_first((k // 4) * NC + (k % 4) * 4 + step for k in range(MEMBERS)):
                if o:
                    give_back(1, ret, me ^ o)
        ret[me] = back[me]

    def receive(l, ret):
        wait_for(ret, ND - 1, ret_sems.at[l])
        for t in range(8):
            stage[t * 256 : (t + 1) * 256, :] = ret[t * 16 : (t + 1) * 16].astype(F32).reshape(256, C)

    def normed_out(l, s):
        return norm_rows(stage[pl.ds(s, C, stride=16), :], cols[l, 1, 0], cols[l, 1, 1])

    loads[0].wait()
    turn_weights(0)
    loads[1].wait()
    for t in range(8):
        first(t)
    project(0, 0)
    pl.semaphore_wait(barrier, MEMBERS - 1 + GROUPS - 1)
    for g in range(1, GROUPS):
        pl.semaphore_signal(in_sems.at[g], inc=1, device_id=place(me ^ group_bits(g)), device_id_type=MESH)
    send_group(0, 0, recv0)
    for g in range(1, GROUPS):
        project(0, g)
        pl.semaphore_wait(in_sems.at[g], 1)
        send_group(0, g, recv0)
    loads[2].wait()
    for l in range(2):
        w_out_t[l] = w_out[l].T
    w_gate_t[...] = w_in[0, :, 4 * C :].T
    for t in range(CHUNKS):
        gate[t] = jax.nn.sigmoid(dot(w_gate_t[...], normed[:, t * C : (t + 1) * C], NN))
    turn_weights(1)
    combine_outgoing(recv0, ret0)
    wait_for(send, ND - 1, send_sems.at[0])
    receive(0, ret0)

    for s in range(CHUNKS):
        v = x[s] + gate[s] * dot(w_out_t[0], normed_out(0, s), NN)
        x[s] = v
        normed[:, s * C : (s + 1) * C] = norm_rows(v, cols[1, 0, 0], cols[1, 0, 1])
    for g in range(GROUPS):
        project(1, g)
        send_group(1, g, recv1)
    for s in range(CHUNKS):
        x_pos[s] = x[s].T
        gate[s] = jax.nn.sigmoid(dot(normed[:, s * C : (s + 1) * C], w_in[1, :, 4 * C :], TN))
    wait_for(back, ND - 1, back_sems.at[0])
    combine_incoming(recv1, ret1)
    wait_for(send, ND - 1, send_sems.at[1])
    receive(1, ret1)
    wait_for(back, ND - 1, back_sems.at[1])

    for s in range(CHUNKS):
        res = x_pos[s] + gate[s] * dot(normed_out(1, s), w_out[1], TN)
        for h in range(2):
            out[pl.ds(h * 16 + s, ROWS, stride=COLS), :] = res[h * ROWS : (h + 1) * ROWS]


def body(pair, token_mask, norm_gains, norm_biases, in_weights, out_weights):
    vmem = pl.BlockSpec(memory_space=pltpu.VMEM)
    hbm = pl.BlockSpec(memory_space=pltpu.HBM)
    res = pl.pallas_call(
        kernel,
        out_shape=jax.ShapeDtypeStruct((ROWS * COLS, C), F32),
        in_specs=[hbm] * 7,
        out_specs=vmem,
        scratch_shapes=[
            pltpu.VMEM((2048, C), F32),
            pltpu.SMEM((512,), jnp.int32),
            pltpu.VMEM((4, C), jnp.int32),
            pltpu.VMEM((4, C), F32),
            pltpu.VMEM((4, C), F32),
            pltpu.VMEM((2, C, 5 * C), BF16),
            pltpu.VMEM((2, C, C), BF16),
            pltpu.VMEM((CHUNKS, C, C), F32),
            pltpu.VMEM((CHUNKS, C, C), F32),
            pltpu.VMEM((C, 2048), BF16),
            pltpu.VMEM((CHUNKS, C, C), F32),
            pltpu.VMEM((2, GROUPS, C, C), BF16),
            pltpu.VMEM((C, C), BF16),
            pltpu.VMEM((2, C, C), BF16),
            pltpu.VMEM((8, 1, 256), F32),
            pltpu.VMEM((2, 2, 2, C, C), F32),
            pltpu.VMEM((ND, 32, C), BF16),
            pltpu.VMEM((ND, 32, C), BF16),
            pltpu.VMEM((ND, 32, C), BF16),
            pltpu.VMEM((ND, 16, C), BF16),
            pltpu.VMEM((ND, 16, C), BF16),
            pltpu.VMEM((ND, 16, C), BF16),
            pltpu.VMEM((2048, C), F32),
            pltpu.VMEM((NC, 32, 512), BF16),
            pltpu.VMEM((NC, 32, 512), BF16),
            pltpu.VMEM((2048, C), F32),
            pltpu.SemaphoreType.DMA((7,)),
            pltpu.SemaphoreType.REGULAR((GROUPS,)),
            pltpu.SemaphoreType.DMA((2,)),
            pltpu.SemaphoreType.DMA((2, GROUPS)),
            pltpu.SemaphoreType.DMA((2,)),
            pltpu.SemaphoreType.DMA((2,)),
        ],
        compiler_params=pltpu.CompilerParams(
            collective_id=0, has_side_effects=True, vmem_limit_bytes=48 << 20),
    )(
        pair.reshape(ROWS * COLS, C), token_mask, token_mask.reshape(4, C),
        norm_gains.reshape(4, C), norm_biases.reshape(4, C), in_weights, out_weights,
    )
    return res.reshape(ROWS, COLS, C)


def solution(mesh):
    placed = (P("row", "col", None), P(), P(), P(), P(), P())
    return jax.shard_map(
        body, mesh=mesh, in_specs=placed, out_specs=P("row", "col", None), check_vma=False
    )
```

```python
import jax
import jax.numpy as jnp
from jax import lax
from jax.experimental import pallas as pl
from jax.experimental.pallas import tpu as pltpu
from jax.sharding import PartitionSpec as P

MESH = pl.DeviceIdType.MESH
F32, BF16 = jnp.float32, jnp.bfloat16
C = 128
ROWS, COLS = 64, 32
NR, NC = 8, 16
ND = NR * NC
CHUNKS = 16
GROUPS = 4
MEMBERS = ND // GROUPS
TN = (((0,), (0,)), ((), ()))
NT = (((1,), (1,)), ((), ()))
NN = (((1,), (0,)), ((), ()))


def dot(a, b, dims):
    return lax.dot_general(a, b, dims, preferred_element_type=F32)


def place(device):
    return (device >> 4, device & 15)


def hops(o):
    return sum((0, 1, 2, 1)[(o >> hi & 1) * 2 + (o >> lo & 1)] for hi, lo in ((3, 6), (5, 4), (2, 1)))


def group_bits(g):
    return (g // 2) * 64 + (g % 2) * 16


def far_first(offsets):
    offsets = list(offsets)
    mixed = [offsets[(7 * k) % len(offsets)] for k in range(len(offsets))]
    return sorted(mixed, key=lambda o: -hops(o))


def group_offsets(l, g):
    if l == 0:
        members = [group_bits(g) + (k // 16) * 32 + k % 16 for k in range(MEMBERS)]
    else:
        members = [(k // 4) * 16 + (k // 2 % 2) * 8 + (k // 2 % 2 ^ g % 2) * 4 + (g // 2) * 2 + k % 2
                   for k in range(MEMBERS)]
    return [o for o in far_first(members) if o]


def slot(l, d):
    if l == 0:
        return d
    b = ((d >> 3) ^ (d >> 2)) & 1
    return ((d >> 1) & 1) * 64 + b * 32 + (d >> 4) * 4 + ((d >> 3) & 1) * 2 + (d & 1)


def norm_rows(v, gain, bias):
    mean = jnp.mean(v, axis=0, keepdims=True)
    centred = v - mean
    var = jnp.mean(centred * centred, axis=0, keepdims=True)
    return (centred * lax.rsqrt(var + 1e-05) * gain + bias).astype(BF16)


def kernel(pair_hbm, mask_hbm, rows_hbm, gains_hbm, biases_hbm, w_in_hbm, w_out_hbm, out,
           pair, mask_smem, mask_vmem, gains, biases, w_in, w_out, x, x_pos, normed, gate, w_t, w_gate_t, w_out_t, mask, cols,
           send, recv0, recv1, back, ret0, ret1, stage, m_left, m_right, wide,
           load_sems, in_sems, send_sems, recv_sems, back_sems, ret_sems):
    r, q = lax.axis_index("row"), lax.axis_index("col")
    me = r * NC + q
    b0, y0 = ((q >> 3) ^ (q >> 2)) & 1, (q >> 1) & 1
    quarters = ((r >> 2) * 2 + (r & 1), y0 * 2 + b0)

    barrier = pltpu.get_barrier_semaphore()
    loads = [
        pltpu.make_async_copy(w_in_hbm, w_in, load_sems.at[0]),
        pltpu.make_async_copy(pair_hbm, pair, load_sems.at[1]),
        pltpu.make_async_copy(w_out_hbm, w_out, load_sems.at[2]),
        pltpu.make_async_copy(mask_hbm, mask_smem, load_sems.at[3]),
        pltpu.make_async_copy(rows_hbm, mask_vmem, load_sems.at[4]),
        pltpu.make_async_copy(gains_hbm, gains, load_sems.at[5]),
        pltpu.make_async_copy(biases_hbm, biases, load_sems.at[6]),
    ]
    for load in loads:
        load.start()
    for o in group_offsets(0, 0) + [group_bits(g) for g in range(1, GROUPS)]:
        pl.semaphore_signal(barrier, inc=1, device_id=place(me ^ o), device_id_type=MESH)

    for load in loads[3:]:
        load.wait()
    low = lax.broadcasted_iota(jnp.int32, (1, C), 1) < ROWS
    pair_rows = mask_vmem[pl.ds(r >> 1, 1), :].astype(F32)
    turned = pltpu.roll(pair_rows, ROWS, 1)
    mine = jnp.where((r & 1) == 0, pair_rows, turned)
    row_mask = jnp.where(low, mine, pltpu.roll(mine, ROWS, 1))
    for s in range(CHUNKS):
        a = mask_smem[q * COLS + s].astype(F32)
        b = mask_smem[q * COLS + CHUNKS + s].astype(F32)
        mask[s // 2, :, (s % 2) * C : (s % 2 + 1) * C] = row_mask * jnp.where(low, a, b)

    def turn_norm(l, i):
        if True:
            cols[l, i, 0] = jnp.broadcast_to(gains[2 * l + i : 2 * l + i + 1, :], (C, C)).T
            cols[l, i, 1] = jnp.broadcast_to(biases[2 * l + i : 2 * l + i + 1, :], (C, C)).T

    def turn_weights(l):
        for part in range(4):
            t = w_in[l, :, part * C : (part + 1) * C].T
            if l == 0:
                for d in range(8):
                    at = part * 32 + (d // 2 % 2) * 16
                    w_t[l, (d // 4) * 2 + d % 2, at : at + 16, :] = t[d * 16 : (d + 1) * 16, :]
            else:
                for g in range(4):
                    w_t[l, g, part * 32 : (part + 1) * 32, :] = t[g * 32 : (g + 1) * 32, :]

    def first(t):
        for e in range(2):
            s = 2 * t + e
            pieces = [pair[pl.ds(h * 16 + s, ROWS, stride=COLS), :] for h in range(2)]
            v = jnp.concatenate(pieces, axis=0).T
            x[s] = v
            normed[:, s * C : (s + 1) * C] = norm_rows(v, cols[0, 0, 0], cols[0, 0, 1])

    def project(l, g):
        part = quarters[l] ^ g
        w = w_t[l, part]
        base = (g % 2) * 1024
        for t in range(8):
            res = dot(w, normed[:, t * 256 : (t + 1) * 256], NN)
            for side in range(2):
                value = res[side * 32 : (side + 1) * 32]
                gated = res[64 + side * 32 : 64 + (side + 1) * 32]
                both = value * jax.nn.sigmoid(gated) * mask[t]
                for e in range(2):
                    wide[pl.ds(base + side * 16 + 2 * t + e, 32, stride=32), :] = both[:, e * C : (e + 1) * C]
        for i in range(4):
            if l == 0:
                at = (part >> 1) * 64 + (part & 1) * 16 + (i // 2) * 32 + (i % 2) * 8
            else:
                at = part * 32 + i * 8
            rows = wide[base + i * 256 : base + (i + 1) * 256, :]
            send[pl.ds(at, 8)] = rows.astype(BF16).reshape(8, 32, C)

    def send_groups(l, groups, recv):
        for o, g in sorted([(o, g) for g in groups for o in group_offsets(l, g)], key=lambda e: -hops(e[0])):
            peer = me ^ o
            pltpu.make_async_remote_copy(
                src_ref=send.at[slot(l, peer)], dst_ref=recv.at[me],
                send_sem=send_sems.at[l], recv_sem=recv_sems.at[l, g],
                device_id=place(peer), device_id_type=MESH).start()
        if 0 in groups:
            recv[me] = send[slot(l, me)]

    def wait_for(ref, count, sem):
        part = ref.at[pl.ds(0, count)]
        pltpu.make_async_copy(part, part, sem).wait()

    def rows_of(g):
        ra = (r ^ ((g // 2) * 4 + g % 2)) & 5
        return ra, ra + 2

    def give_back(l, ret, peer):
        pltpu.make_async_remote_copy(
            src_ref=back.at[peer], dst_ref=ret.at[slot(l, me)],
            send_sem=back_sems.at[l], recv_sem=ret_sems.at[l],
            device_id=place(peer), device_id_type=MESH).start()

    def assemble(recv, ra, rb, c, at, lanes):
        t0 = recv[ra * NC + c].astype(F32)
        t1 = recv[rb * NC + c].astype(F32)
        a = jnp.where(low, t0, pltpu.roll(t1, ROWS, 1)).astype(BF16)
        b = jnp.where(low, pltpu.roll(t0, ROWS, 1), t1).astype(BF16)
        m_left[at, 0:16, lanes] = a[0:16]
        m_left[at, 16:32, lanes] = b[0:16]
        m_right[at, 0:16, lanes] = a[16:32]
        m_right[at, 16:32, lanes] = b[16:32]

    def pack(tile, ra, rb, tq):
        x0, x1 = tile[0:16], tile[16:32]
        back[ra * NC + tq] = jnp.where(low, x0, pltpu.roll(x1, ROWS, 1)).astype(BF16)
        back[rb * NC + tq] = jnp.where(low, pltpu.roll(x0, ROWS, 1), x1).astype(BF16)

    def combine_outgoing(recv, ret):
        for g in range(GROUPS):
            wait_for(recv, MEMBERS - (g == 0), recv_sems.at[0, g])
            lanes = slice(g * C, (g + 1) * C)
            ra, rb = rows_of(g)
            for c in range(NC):
                assemble(recv, ra, rb, c, c, lanes)
            right = m_right[:, :, lanes].reshape(512, C)
            res = dot(right, m_left[:, :, : (g + 1) * C].reshape(512, (g + 1) * C), TN)
            blocks = {(g, gi): res[:, gi * C : (gi + 1) * C] for gi in range(g + 1)}
            if g:
                left = m_left[:, :, lanes].reshape(512, C)
                res = dot(m_right[:, :, : g * C].reshape(512, g * C), left, TN)
                blocks.update({(gj, g): res[gj * C : (gj + 1) * C] for gj in range(g)})
            for (gj, gi), block in blocks.items():
                jr, (ra, rb) = rows_of(gj)[0], rows_of(gi)
                for jh in range(2):
                    for jq in range(2):
                        at = jh * 64 + jq * 32
                        pack(block[at : at + 32], ra, rb, (jr >> 2) * 8 + jh * 4 + (jr & 1) * 2 + jq)
        for o in far_first(range(1, ND)):
            give_back(0, ret, me ^ o)
        ret[me] = back[me]

    def combine_incoming(recv, ret):
        def label(g):
            return b0 ^ (g % 2), y0 ^ (g // 2)

        def column(g, x, core):
            b, y = label(g)
            return x * 8 + (b ^ x) * 4 + y * 2 + core

        for g in range(GROUPS):
            wait_for(recv, MEMBERS - (g == 0), recv_sems.at[1, g])
            for x in range(2):
                for core in range(2):
                    for p in range(4):
                        assemble(recv, 2 * p, 2 * p + 1, column(g, x, core), g * 4 + x * 2 + core,
                                 slice(p * C, (p + 1) * C))
            right = m_right[g * 4 : (g + 1) * 4].reshape(C, 512)
            res = dot(right, m_left[: (g + 1) * 4].reshape((g + 1) * C, 512), NT)
            blocks = {(g, gi): res[:, gi * C : (gi + 1) * C] for gi in range(g + 1)}
            if g:
                left = m_left[g * 4 : (g + 1) * 4].reshape(C, 512)
                res = dot(m_right[: g * 4].reshape(g * C, 512), left, NT)
                blocks.update({(gj, g): res[gj * C : (gj + 1) * C] for gj in range(g)})
            sends = []
            for (gj, gi), block in blocks.items():
                b, y = label(gi)
                for x in range(2):
                    for core in range(2):
                        at = (x * 2 + core) * 32
                        pack(block[at : at + 32], b * 2 + y, 4 + (b ^ 1) * 2 + y, column(gj, x, core))
                for xr in range(2):
                    tr = (r >> 2) ^ xr
                    tr = tr * 4 + (tr ^ b) * 2 + y
                    for k in range(4):
                        o = (k // 2) * 8 + (k // 2 ^ gj % 2) * 4 + (gj // 2) * 2 + k % 2
                        sends.append((hops(o & 6) + k // 2, tr * NC + (q ^ o)))
            for _, peer in sorted(sends, key=lambda e: -e[0]):
                @pl.when(peer != me)
                def _(peer=peer):
                    give_back(1, ret, peer)
        ret[slot(1, me)] = back[me]

    def receive(l, ret):
        wait_for(ret, ND - 1, ret_sems.at[l])
        for t in range(8):
            stage[t * 256 : (t + 1) * 256, :] = ret[t * 16 : (t + 1) * 16].astype(F32).reshape(256, C)

    def normed_out(l, s):
        return norm_rows(stage[pl.ds(s, C, stride=16), :], cols[l, 1, 0], cols[l, 1, 1])

    turn_norm(0, 0)
    loads[0].wait()
    turn_weights(0)
    loads[1].wait()
    for t in range(8):
        first(t)
    project(0, 0)
    pl.semaphore_wait(barrier, MEMBERS - 1 + GROUPS - 1)
    for g in range(1, GROUPS):
        pl.semaphore_signal(in_sems.at[g], inc=1, device_id=place(me ^ group_bits(g)), device_id_type=MESH)
    send_groups(0, (0,), recv0)
    for g in range(1, GROUPS):
        project(0, g)
        pl.semaphore_wait(in_sems.at[g], 1)
        send_groups(0, (g,), recv0)
    loads[2].wait()
    for l, i in ((0, 1), (1, 0), (1, 1)):
        turn_norm(l, i)
    for l in range(2):
        w_out_t[l] = w_out[l].T
    w_gate_t[...] = w_in[0, :, 4 * C :].T
    for t in range(CHUNKS):
        gate[t] = jax.nn.sigmoid(dot(w_gate_t[...], normed[:, t * C : (t + 1) * C], NN))
    turn_weights(1)
    combine_outgoing(recv0, ret0)
    wait_for(send, ND - 1, send_sems.at[0])
    receive(0, ret0)

    for s in range(CHUNKS):
        v = x[s] + gate[s] * dot(w_out_t[0], normed_out(0, s), NN)
        x[s] = v
        normed[:, s * C : (s + 1) * C] = norm_rows(v, cols[1, 0, 0], cols[1, 0, 1])
    for g in range(0, GROUPS, 2):
        project(1, g)
        project(1, g + 1)
        send_groups(1, (g, g + 1), recv1)
    for s in range(CHUNKS):
        x_pos[s] = x[s].T
        gate[s] = jax.nn.sigmoid(dot(normed[:, s * C : (s + 1) * C], w_in[1, :, 4 * C :], TN))
    wait_for(back, ND - 1, back_sems.at[0])
    combine_incoming(recv1, ret1)
    wait_for(send, ND - 1, send_sems.at[1])
    receive(1, ret1)
    wait_for(back, ND - 1, back_sems.at[1])

    for s in range(CHUNKS):
        res = x_pos[s] + gate[s] * dot(normed_out(1, s), w_out[1], TN)
        for h in range(2):
            out[pl.ds(h * 16 + s, ROWS, stride=COLS), :] = res[h * ROWS : (h + 1) * ROWS]


def body(pair, token_mask, norm_gains, norm_biases, in_weights, out_weights):
    vmem = pl.BlockSpec(memory_space=pltpu.VMEM)
    hbm = pl.BlockSpec(memory_space=pltpu.HBM)
    res = pl.pallas_call(
        kernel,
        out_shape=jax.ShapeDtypeStruct((ROWS * COLS, C), F32),
        in_specs=[hbm] * 7,
        out_specs=vmem,
        scratch_shapes=[
            pltpu.VMEM((2048, C), F32),
            pltpu.SMEM((512,), jnp.int32),
            pltpu.VMEM((4, C), jnp.int32),
            pltpu.VMEM((4, C), F32),
            pltpu.VMEM((4, C), F32),
            pltpu.VMEM((2, C, 5 * C), BF16),
            pltpu.VMEM((2, C, C), BF16),
            pltpu.VMEM((CHUNKS, C, C), F32),
            pltpu.VMEM((CHUNKS, C, C), F32),
            pltpu.VMEM((C, 2048), BF16),
            pltpu.VMEM((CHUNKS, C, C), F32),
            pltpu.VMEM((2, GROUPS, C, C), BF16),
            pltpu.VMEM((C, C), BF16),
            pltpu.VMEM((2, C, C), BF16),
            pltpu.VMEM((8, 1, 256), F32),
            pltpu.VMEM((2, 2, 2, C, C), F32),
            pltpu.VMEM((ND, 32, C), BF16),
            pltpu.VMEM((ND, 32, C), BF16),
            pltpu.VMEM((ND, 32, C), BF16),
            pltpu.VMEM((ND, 16, C), BF16),
            pltpu.VMEM((ND, 16, C), BF16),
            pltpu.VMEM((ND, 16, C), BF16),
            pltpu.VMEM((2048, C), F32),
            pltpu.VMEM((NC, 32, 512), BF16),
            pltpu.VMEM((NC, 32, 512), BF16),
            pltpu.VMEM((2048, C), F32),
            pltpu.SemaphoreType.DMA((7,)),
            pltpu.SemaphoreType.REGULAR((GROUPS,)),
            pltpu.SemaphoreType.DMA((2,)),
            pltpu.SemaphoreType.DMA((2, GROUPS)),
            pltpu.SemaphoreType.DMA((2,)),
            pltpu.SemaphoreType.DMA((2,)),
        ],
        compiler_params=pltpu.CompilerParams(
            collective_id=0, has_side_effects=True, vmem_limit_bytes=48 << 20),
    )(
        pair.reshape(ROWS * COLS, C), token_mask, token_mask.reshape(4, C),
        norm_gains.reshape(4, C), norm_biases.reshape(4, C), in_weights, out_weights,
    )
    return res.reshape(ROWS, COLS, C)


def solution(mesh):
    placed = (P("row", "col", None), P(), P(), P(), P(), P())
    return jax.shard_map(
        body, mesh=mesh, in_specs=placed, out_specs=P("row", "col", None), check_vma=False
    )
```

```python
import jax
import jax.numpy as jnp
from jax import lax
from jax.experimental import pallas as pl
from jax.experimental.pallas import tpu as pltpu
from jax.sharding import PartitionSpec as P

MESH = pl.DeviceIdType.MESH
F32, BF16 = jnp.float32, jnp.bfloat16
C = 128
ROWS, COLS = 64, 32
NR, NC = 8, 16
ND = NR * NC
CHUNKS = 16
GROUPS = 4
MEMBERS = ND // GROUPS
TN = (((0,), (0,)), ((), ()))
NT = (((1,), (1,)), ((), ()))
NN = (((1,), (0,)), ((), ()))


def dot(a, b, dims):
    return lax.dot_general(a, b, dims, preferred_element_type=F32)


def place(device):
    return (device >> 4, device & 15)


def hops(o):
    return sum((0, 1, 2, 1)[(o >> hi & 1) * 2 + (o >> lo & 1)] for hi, lo in ((3, 6), (5, 4), (2, 1)))


def group_bits(g):
    return (g // 2) * 64 + (g % 2) * 16


def far_first(offsets):
    offsets = list(offsets)
    mixed = [offsets[(5 * k) % len(offsets)] for k in range(len(offsets))]
    return sorted(mixed, key=lambda o: -hops(o))


def group_offsets(l, g):
    if l == 0:
        members = [group_bits(g) + (k // 16) * 32 + k % 16 for k in range(MEMBERS)]
    else:
        members = [(k // 4) * 16 + (k // 2 % 2) * 8 + (k // 2 % 2 ^ g % 2) * 4 + (g // 2) * 2 + k % 2
                   for k in range(MEMBERS)]
    return [o for o in far_first(members) if o]


def slot(l, d):
    if l == 0:
        return d
    b = ((d >> 3) ^ (d >> 2)) & 1
    return ((d >> 1) & 1) * 64 + b * 32 + (d >> 4) * 4 + ((d >> 3) & 1) * 2 + (d & 1)


def norm_rows(v, gain, bias):
    mean = jnp.mean(v, axis=0, keepdims=True)
    centred = v - mean
    var = jnp.mean(centred * centred, axis=0, keepdims=True)
    return (centred * lax.rsqrt(var + 1e-05) * gain + bias).astype(BF16)


def kernel(pair_hbm, mask_hbm, rows_hbm, gains_hbm, biases_hbm, w_in_hbm, w_out_hbm, out,
           pair, mask_smem, mask_vmem, gains, biases, w_in, w_out, x, x_pos, normed, gate, w_t, w_gate_t, w_out_t, mask, cols,
           send, recv0, recv1, back, ret0, ret1, stage, m_left, m_right, wide,
           load_sems, in_sems, send_sems, recv_sems, back_sems, ret_sems):
    r, q = lax.axis_index("row"), lax.axis_index("col")
    me = r * NC + q
    b0, y0 = ((q >> 3) ^ (q >> 2)) & 1, (q >> 1) & 1
    quarters = ((r >> 2) * 2 + (r & 1), y0 * 2 + b0)

    barrier = pltpu.get_barrier_semaphore()
    loads = [
        pltpu.make_async_copy(w_in_hbm, w_in, load_sems.at[0]),
        pltpu.make_async_copy(pair_hbm, pair, load_sems.at[1]),
        pltpu.make_async_copy(w_out_hbm, w_out, load_sems.at[2]),
        pltpu.make_async_copy(mask_hbm, mask_smem, load_sems.at[3]),
        pltpu.make_async_copy(rows_hbm, mask_vmem, load_sems.at[4]),
        pltpu.make_async_copy(gains_hbm, gains, load_sems.at[5]),
        pltpu.make_async_copy(biases_hbm, biases, load_sems.at[6]),
    ]
    for load in loads:
        load.start()
    for o in group_offsets(0, 0) + [group_bits(g) for g in range(1, GROUPS)]:
        pl.semaphore_signal(barrier, inc=1, device_id=place(me ^ o), device_id_type=MESH)

    for load in loads[3:]:
        load.wait()
    low = lax.broadcasted_iota(jnp.int32, (1, C), 1) < ROWS
    pair_rows = mask_vmem[pl.ds(r >> 1, 1), :].astype(F32)
    turned = pltpu.roll(pair_rows, ROWS, 1)
    mine = jnp.where((r & 1) == 0, pair_rows, turned)
    row_mask = jnp.where(low, mine, pltpu.roll(mine, ROWS, 1))
    for s in range(CHUNKS):
        a = mask_smem[q * COLS + s].astype(F32)
        b = mask_smem[q * COLS + CHUNKS + s].astype(F32)
        mask[s // 2, :, (s % 2) * C : (s % 2 + 1) * C] = row_mask * jnp.where(low, a, b)

    def turn_norm(l, i):
        if True:
            cols[l, i, 0] = jnp.broadcast_to(gains[2 * l + i : 2 * l + i + 1, :], (C, C)).T
            cols[l, i, 1] = jnp.broadcast_to(biases[2 * l + i : 2 * l + i + 1, :], (C, C)).T

    def turn_weights(l):
        for part in range(4):
            t = w_in[l, :, part * C : (part + 1) * C].T
            if l == 0:
                for d in range(8):
                    at = part * 32 + (d // 2 % 2) * 16
                    w_t[l, (d // 4) * 2 + d % 2, at : at + 16, :] = t[d * 16 : (d + 1) * 16, :]
            else:
                for g in range(4):
                    w_t[l, g, part * 32 : (part + 1) * 32, :] = t[g * 32 : (g + 1) * 32, :]

    def first(t):
        for e in range(2):
            s = 2 * t + e
            pieces = [pair[pl.ds(h * 16 + s, ROWS, stride=COLS), :] for h in range(2)]
            v = jnp.concatenate(pieces, axis=0).T
            x[s] = v
            normed[:, s * C : (s + 1) * C] = norm_rows(v, cols[0, 0, 0], cols[0, 0, 1])

    def project(l, g):
        part = quarters[l] ^ g
        w = w_t[l, part]
        base = (g % 2) * 1024
        for t in range(8):
            res = dot(w, normed[:, t * 256 : (t + 1) * 256], NN)
            for side in range(2):
                value = res[side * 32 : (side + 1) * 32]
                gated = res[64 + side * 32 : 64 + (side + 1) * 32]
                both = value * jax.nn.sigmoid(gated) * mask[t]
                for e in range(2):
                    wide[pl.ds(base + side * 16 + 2 * t + e, 32, stride=32), :] = both[:, e * C : (e + 1) * C]
        for i in range(4):
            if l == 0:
                at = (part >> 1) * 64 + (part & 1) * 16 + (i // 2) * 32 + (i % 2) * 8
            else:
                at = part * 32 + i * 8
            rows = wide[base + i * 256 : base + (i + 1) * 256, :]
            send[pl.ds(at, 8)] = rows.astype(BF16).reshape(8, 32, C)

    def send_groups(l, groups, recv):
        for o, g in sorted([(o, g) for g in groups for o in group_offsets(l, g)], key=lambda e: -hops(e[0])):
            peer = me ^ o
            pltpu.make_async_remote_copy(
                src_ref=send.at[slot(l, peer)], dst_ref=recv.at[me],
                send_sem=send_sems.at[l], recv_sem=recv_sems.at[l, g],
                device_id=place(peer), device_id_type=MESH).start()
        if 0 in groups:
            recv[me] = send[slot(l, me)]

    def wait_for(ref, count, sem):
        part = ref.at[pl.ds(0, count)]
        pltpu.make_async_copy(part, part, sem).wait()

    def rows_of(g):
        ra = (r ^ ((g // 2) * 4 + g % 2)) & 5
        return ra, ra + 2

    def give_back(l, ret, peer):
        pltpu.make_async_remote_copy(
            src_ref=back.at[peer], dst_ref=ret.at[slot(l, me)],
            send_sem=back_sems.at[l], recv_sem=ret_sems.at[l],
            device_id=place(peer), device_id_type=MESH).start()

    def assemble(recv, ra, rb, c, at, lanes):
        t0 = recv[ra * NC + c].astype(F32)
        t1 = recv[rb * NC + c].astype(F32)
        a = jnp.where(low, t0, pltpu.roll(t1, ROWS, 1)).astype(BF16)
        b = jnp.where(low, pltpu.roll(t0, ROWS, 1), t1).astype(BF16)
        m_left[at, 0:16, lanes] = a[0:16]
        m_left[at, 16:32, lanes] = b[0:16]
        m_right[at, 0:16, lanes] = a[16:32]
        m_right[at, 16:32, lanes] = b[16:32]

    def pack(tile, ra, rb, tq):
        x0, x1 = tile[0:16], tile[16:32]
        back[ra * NC + tq] = jnp.where(low, x0, pltpu.roll(x1, ROWS, 1)).astype(BF16)
        back[rb * NC + tq] = jnp.where(low, pltpu.roll(x0, ROWS, 1), x1).astype(BF16)

    def combine_outgoing(recv, ret):
        for g in range(GROUPS):
            wait_for(recv, MEMBERS - (g == 0), recv_sems.at[0, g])
            lanes = slice(g * C, (g + 1) * C)
            ra, rb = rows_of(g)
            for c in range(NC):
                assemble(recv, ra, rb, c, c, lanes)
            right = m_right[:, :, lanes].reshape(512, C)
            res = dot(right, m_left[:, :, : (g + 1) * C].reshape(512, (g + 1) * C), TN)
            blocks = {(g, gi): res[:, gi * C : (gi + 1) * C] for gi in range(g + 1)}
            if g:
                left = m_left[:, :, lanes].reshape(512, C)
                res = dot(m_right[:, :, : g * C].reshape(512, g * C), left, TN)
                blocks.update({(gj, g): res[gj * C : (gj + 1) * C] for gj in range(g)})
            for (gj, gi), block in blocks.items():
                jr, (ra, rb) = rows_of(gj)[0], rows_of(gi)
                for jh in range(2):
                    for jq in range(2):
                        at = jh * 64 + jq * 32
                        pack(block[at : at + 32], ra, rb, (jr >> 2) * 8 + jh * 4 + (jr & 1) * 2 + jq)
        for o in far_first(range(1, ND)):
            give_back(0, ret, me ^ o)
        ret[me] = back[me]

    def combine_incoming(recv, ret):
        def label(g):
            return b0 ^ (g % 2), y0 ^ (g // 2)

        def column(g, x, core):
            b, y = label(g)
            return x * 8 + (b ^ x) * 4 + y * 2 + core

        for g in range(GROUPS):
            wait_for(recv, MEMBERS - (g == 0), recv_sems.at[1, g])
            for x in range(2):
                for core in range(2):
                    for p in range(4):
                        assemble(recv, 2 * p, 2 * p + 1, column(g, x, core), g * 4 + x * 2 + core,
                                 slice(p * C, (p + 1) * C))
            right = m_right[g * 4 : (g + 1) * 4].reshape(C, 512)
            res = dot(right, m_left[: (g + 1) * 4].reshape((g + 1) * C, 512), NT)
            blocks = {(g, gi): res[:, gi * C : (gi + 1) * C] for gi in range(g + 1)}
            if g:
                left = m_left[g * 4 : (g + 1) * 4].reshape(C, 512)
                res = dot(m_right[: g * 4].reshape(g * C, 512), left, NT)
                blocks.update({(gj, g): res[gj * C : (gj + 1) * C] for gj in range(g)})
            sends = []
            for (gj, gi), block in blocks.items():
                b, y = label(gi)
                for x in range(2):
                    for core in range(2):
                        at = (x * 2 + core) * 32
                        pack(block[at : at + 32], b * 2 + y, 4 + (b ^ 1) * 2 + y, column(gj, x, core))
                for xr in range(2):
                    tr = (r >> 2) ^ xr
                    tr = tr * 4 + (tr ^ b) * 2 + y
                    for k in range(4):
                        o = (k // 2) * 8 + (k // 2 ^ gj % 2) * 4 + (gj // 2) * 2 + k % 2
                        sends.append((hops(o & 6) + k // 2, tr * NC + (q ^ o)))
            for _, peer in sorted(sends, key=lambda e: -e[0]):
                @pl.when(peer != me)
                def _(peer=peer):
                    give_back(1, ret, peer)
        ret[slot(1, me)] = back[me]

    def receive(l, ret):
        wait_for(ret, ND - 1, ret_sems.at[l])
        for t in range(8):
            stage[t * 256 : (t + 1) * 256, :] = ret[t * 16 : (t + 1) * 16].astype(F32).reshape(256, C)

    def normed_out(l, s):
        return norm_rows(stage[pl.ds(s, C, stride=16), :], cols[l, 1, 0], cols[l, 1, 1])

    turn_norm(0, 0)
    loads[0].wait()
    turn_weights(0)
    loads[1].wait()
    for t in range(8):
        first(t)
    project(0, 0)
    pl.semaphore_wait(barrier, MEMBERS - 1 + GROUPS - 1)
    for g in range(1, GROUPS):
        pl.semaphore_signal(in_sems.at[g], inc=1, device_id=place(me ^ group_bits(g)), device_id_type=MESH)
    send_groups(0, (0,), recv0)
    project(0, 1)
    pl.semaphore_wait(in_sems.at[1], 1)
    send_groups(0, (1,), recv0)
    project(0, 2)
    project(0, 3)
    pl.semaphore_wait(in_sems.at[2], 1)
    pl.semaphore_wait(in_sems.at[3], 1)
    send_groups(0, (2, 3), recv0)
    loads[2].wait()
    for l, i in ((0, 1), (1, 0), (1, 1)):
        turn_norm(l, i)
    for l in range(2):
        w_out_t[l] = w_out[l].T
    w_gate_t[...] = w_in[0, :, 4 * C :].T
    for t in range(CHUNKS):
        gate[t] = jax.nn.sigmoid(dot(w_gate_t[...], normed[:, t * C : (t + 1) * C], NN))
    turn_weights(1)
    combine_outgoing(recv0, ret0)
    wait_for(send, ND - 1, send_sems.at[0])
    receive(0, ret0)

    for s in range(CHUNKS):
        v = x[s] + gate[s] * dot(w_out_t[0], normed_out(0, s), NN)
        x[s] = v
        normed[:, s * C : (s + 1) * C] = norm_rows(v, cols[1, 0, 0], cols[1, 0, 1])
    for g in range(0, GROUPS, 2):
        project(1, g)
        project(1, g + 1)
        send_groups(1, (g, g + 1), recv1)
    for s in range(CHUNKS):
        x_pos[s] = x[s].T
        gate[s] = jax.nn.sigmoid(dot(normed[:, s * C : (s + 1) * C], w_in[1, :, 4 * C :], TN))
    wait_for(back, ND - 1, back_sems.at[0])
    combine_incoming(recv1, ret1)
    wait_for(send, ND - 1, send_sems.at[1])
    receive(1, ret1)
    wait_for(back, ND - 1, back_sems.at[1])

    for s in range(CHUNKS):
        res = x_pos[s] + gate[s] * dot(normed_out(1, s), w_out[1], TN)
        for h in range(2):
            out[pl.ds(h * 16 + s, ROWS, stride=COLS), :] = res[h * ROWS : (h + 1) * ROWS]


def body(pair, token_mask, norm_gains, norm_biases, in_weights, out_weights):
    vmem = pl.BlockSpec(memory_space=pltpu.VMEM)
    hbm = pl.BlockSpec(memory_space=pltpu.HBM)
    res = pl.pallas_call(
        kernel,
        out_shape=jax.ShapeDtypeStruct((ROWS * COLS, C), F32),
        in_specs=[hbm] * 7,
        out_specs=vmem,
        scratch_shapes=[
            pltpu.VMEM((2048, C), F32),
            pltpu.SMEM((512,), jnp.int32),
            pltpu.VMEM((4, C), jnp.int32),
            pltpu.VMEM((4, C), F32),
            pltpu.VMEM((4, C), F32),
            pltpu.VMEM((2, C, 5 * C), BF16),
            pltpu.VMEM((2, C, C), BF16),
            pltpu.VMEM((CHUNKS, C, C), F32),
            pltpu.VMEM((CHUNKS, C, C), F32),
            pltpu.VMEM((C, 2048), BF16),
            pltpu.VMEM((CHUNKS, C, C), F32),
            pltpu.VMEM((2, GROUPS, C, C), BF16),
            pltpu.VMEM((C, C), BF16),
            pltpu.VMEM((2, C, C), BF16),
            pltpu.VMEM((8, 1, 256), F32),
            pltpu.VMEM((2, 2, 2, C, C), F32),
            pltpu.VMEM((ND, 32, C), BF16),
            pltpu.VMEM((ND, 32, C), BF16),
            pltpu.VMEM((ND, 32, C), BF16),
            pltpu.VMEM((ND, 16, C), BF16),
            pltpu.VMEM((ND, 16, C), BF16),
            pltpu.VMEM((ND, 16, C), BF16),
            pltpu.VMEM((2048, C), F32),
            pltpu.VMEM((NC, 32, 512), BF16),
            pltpu.VMEM((NC, 32, 512), BF16),
            pltpu.VMEM((2048, C), F32),
            pltpu.SemaphoreType.DMA((7,)),
            pltpu.SemaphoreType.REGULAR((GROUPS,)),
            pltpu.SemaphoreType.DMA((2,)),
            pltpu.SemaphoreType.DMA((2, GROUPS)),
            pltpu.SemaphoreType.DMA((2,)),
            pltpu.SemaphoreType.DMA((2,)),
        ],
        compiler_params=pltpu.CompilerParams(
            collective_id=0, has_side_effects=True, vmem_limit_bytes=48 << 20),
    )(
        pair.reshape(ROWS * COLS, C), token_mask, token_mask.reshape(4, C),
        norm_gains.reshape(4, C), norm_biases.reshape(4, C), in_weights, out_weights,
    )
    return res.reshape(ROWS, COLS, C)


def solution(mesh):
    placed = (P("row", "col", None), P(), P(), P(), P(), P())
    return jax.shard_map(
        body, mesh=mesh, in_specs=placed, out_specs=P("row", "col", None), check_vma=False
    )
```

```python
import jax
import jax.numpy as jnp
from jax import lax
from jax.experimental import pallas as pl
from jax.experimental.pallas import tpu as pltpu
from jax.sharding import PartitionSpec as P

MESH = pl.DeviceIdType.MESH
F32, BF16 = jnp.float32, jnp.bfloat16
C = 128
ROWS, COLS = 64, 32
NR, NC = 8, 16
ND = NR * NC
CHUNKS = 16
GROUPS = 4
MEMBERS = ND // GROUPS
TN = (((0,), (0,)), ((), ()))
NT = (((1,), (1,)), ((), ()))
NN = (((1,), (0,)), ((), ()))


def dot(a, b, dims):
    return lax.dot_general(a, b, dims, preferred_element_type=F32)


def place(device):
    return (device >> 4, device & 15)


def hops(o):
    return sum((0, 1, 2, 1)[(o >> hi & 1) * 2 + (o >> lo & 1)] for hi, lo in ((3, 6), (5, 4), (2, 1)))


def group_bits(g):
    return (g // 2) * 64 + (g % 2) * 16


def far_first(offsets):
    offsets = list(offsets)
    mixed = [offsets[(5 * k) % len(offsets)] for k in range(len(offsets))]
    return sorted(mixed, key=lambda o: -hops(o))


def group_offsets(l, g):
    if l == 0:
        members = [group_bits(g) + (k // 16) * 32 + k % 16 for k in range(MEMBERS)]
    else:
        members = [(k // 4) * 16 + (k // 2 % 2) * 8 + (k // 2 % 2 ^ g % 2) * 4 + (g // 2) * 2 + k % 2
                   for k in range(MEMBERS)]
    return [o for o in far_first(members) if o]


def slot(l, d):
    if l == 0:
        return d
    b = ((d >> 3) ^ (d >> 2)) & 1
    return ((d >> 1) & 1) * 64 + b * 32 + (d >> 4) * 4 + ((d >> 3) & 1) * 2 + (d & 1)


def norm_rows(v, gain, bias):
    mean = jnp.mean(v, axis=0, keepdims=True)
    centred = v - mean
    var = jnp.mean(centred * centred, axis=0, keepdims=True)
    return (centred * lax.rsqrt(var + 1e-05) * gain + bias).astype(BF16)


def kernel(pair_hbm, mask_hbm, rows_hbm, gains_hbm, biases_hbm, w_in_hbm, w_out_hbm, out,
           pair, mask_smem, mask_vmem, gains, biases, w_in, w_out, x, x_pos, normed, gate, w_t, w_gate_t, w_out_t, mask, cols,
           send, recv0, recv1, back, ret0, ret1, stage, m_left, m_right, wide,
           load_sems, in_sems, send_sems, recv_sems, back_sems, ret_sems):
    r, q = lax.axis_index("row"), lax.axis_index("col")
    me = r * NC + q
    b0, y0 = ((q >> 3) ^ (q >> 2)) & 1, (q >> 1) & 1
    quarters = ((r >> 2) * 2 + (r & 1), y0 * 2 + b0)

    barrier = pltpu.get_barrier_semaphore()
    loads = [
        pltpu.make_async_copy(w_in_hbm, w_in, load_sems.at[0]),
        pltpu.make_async_copy(pair_hbm, pair, load_sems.at[1]),
        pltpu.make_async_copy(w_out_hbm, w_out, load_sems.at[2]),
        pltpu.make_async_copy(mask_hbm, mask_smem, load_sems.at[3]),
        pltpu.make_async_copy(rows_hbm, mask_vmem, load_sems.at[4]),
        pltpu.make_async_copy(gains_hbm, gains, load_sems.at[5]),
        pltpu.make_async_copy(biases_hbm, biases, load_sems.at[6]),
    ]
    for load in loads:
        load.start()
    for o in group_offsets(0, 0) + [group_bits(g) for g in range(1, GROUPS)]:
        pl.semaphore_signal(barrier, inc=1, device_id=place(me ^ o), device_id_type=MESH)

    for load in loads[3:]:
        load.wait()
    low = lax.broadcasted_iota(jnp.int32, (1, C), 1) < ROWS
    pair_rows = mask_vmem[pl.ds(r >> 1, 1), :].astype(F32)
    turned = pltpu.roll(pair_rows, ROWS, 1)
    mine = jnp.where((r & 1) == 0, pair_rows, turned)
    row_mask = jnp.where(low, mine, pltpu.roll(mine, ROWS, 1))
    for s in range(CHUNKS):
        a = mask_smem[q * COLS + s].astype(F32)
        b = mask_smem[q * COLS + CHUNKS + s].astype(F32)
        mask[s // 2, :, (s % 2) * C : (s % 2 + 1) * C] = row_mask * jnp.where(low, a, b)

    def turn_norm(l, i):
        if True:
            cols[l, i, 0] = jnp.broadcast_to(gains[2 * l + i : 2 * l + i + 1, :], (C, C)).T
            cols[l, i, 1] = jnp.broadcast_to(biases[2 * l + i : 2 * l + i + 1, :], (C, C)).T

    def turn_weights(l):
        for part in range(4):
            t = w_in[l, :, part * C : (part + 1) * C].T
            if l == 0:
                for d in range(8):
                    at = part * 32 + (d // 2 % 2) * 16
                    w_t[l, (d // 4) * 2 + d % 2, at : at + 16, :] = t[d * 16 : (d + 1) * 16, :]
            else:
                for g in range(4):
                    w_t[l, g, part * 32 : (part + 1) * 32, :] = t[g * 32 : (g + 1) * 32, :]

    def first(t):
        for e in range(2):
            s = 2 * t + e
            pieces = [pair[pl.ds(h * 16 + s, ROWS, stride=COLS), :] for h in range(2)]
            v = jnp.concatenate(pieces, axis=0).T
            x[s] = v
            normed[:, s * C : (s + 1) * C] = norm_rows(v, cols[0, 0, 0], cols[0, 0, 1])

    def project(l, g):
        part = quarters[l] ^ g
        w = w_t[l, part]
        base = (g % 2) * 1024
        for t in range(8):
            res = dot(w, normed[:, t * 256 : (t + 1) * 256], NN)
            for side in range(2):
                value = res[side * 32 : (side + 1) * 32]
                gated = res[64 + side * 32 : 64 + (side + 1) * 32]
                both = value * jax.nn.sigmoid(gated) * mask[t]
                for e in range(2):
                    wide[pl.ds(base + side * 16 + 2 * t + e, 32, stride=32), :] = both[:, e * C : (e + 1) * C]
        for i in range(4):
            if l == 0:
                at = (part >> 1) * 64 + (part & 1) * 16 + (i // 2) * 32 + (i % 2) * 8
            else:
                at = part * 32 + i * 8
            rows = wide[base + i * 256 : base + (i + 1) * 256, :]
            send[pl.ds(at, 8)] = rows.astype(BF16).reshape(8, 32, C)

    def send_groups(l, groups, recv):
        for o, g in sorted([(o, g) for g in groups for o in group_offsets(l, g)], key=lambda e: -hops(e[0])):
            peer = me ^ o
            pltpu.make_async_remote_copy(
                src_ref=send.at[slot(l, peer)], dst_ref=recv.at[me],
                send_sem=send_sems.at[l], recv_sem=recv_sems.at[l, g],
                device_id=place(peer), device_id_type=MESH).start()
        if 0 in groups:
            recv[me] = send[slot(l, me)]

    def wait_for(ref, count, sem):
        part = ref.at[pl.ds(0, count)]
        pltpu.make_async_copy(part, part, sem).wait()

    def rows_of(g):
        ra = (r ^ ((g // 2) * 4 + g % 2)) & 5
        return ra, ra + 2

    def give_back(l, ret, peer):
        pltpu.make_async_remote_copy(
            src_ref=back.at[peer], dst_ref=ret.at[slot(l, me)],
            send_sem=back_sems.at[l], recv_sem=ret_sems.at[l],
            device_id=place(peer), device_id_type=MESH).start()

    def assemble(recv, ra, rb, c, at, lanes):
        t0 = recv[ra * NC + c].astype(F32)
        t1 = recv[rb * NC + c].astype(F32)
        a = jnp.where(low, t0, pltpu.roll(t1, ROWS, 1)).astype(BF16)
        b = jnp.where(low, pltpu.roll(t0, ROWS, 1), t1).astype(BF16)
        m_left[at, 0:16, lanes] = a[0:16]
        m_left[at, 16:32, lanes] = b[0:16]
        m_right[at, 0:16, lanes] = a[16:32]
        m_right[at, 16:32, lanes] = b[16:32]

    def pack(tile, ra, rb, tq):
        x0, x1 = tile[0:16], tile[16:32]
        back[ra * NC + tq] = jnp.where(low, x0, pltpu.roll(x1, ROWS, 1)).astype(BF16)
        back[rb * NC + tq] = jnp.where(low, pltpu.roll(x0, ROWS, 1), x1).astype(BF16)

    def combine_outgoing(recv, ret):
        for g in range(GROUPS):
            wait_for(recv, MEMBERS - (g == 0), recv_sems.at[0, g])
            lanes = slice(g * C, (g + 1) * C)
            ra, rb = rows_of(g)
            for c in range(NC):
                assemble(recv, ra, rb, c, c, lanes)
            right = m_right[:, :, lanes].reshape(512, C)
            res = dot(right, m_left[:, :, : (g + 1) * C].reshape(512, (g + 1) * C), TN)
            blocks = {(g, gi): res[:, gi * C : (gi + 1) * C] for gi in range(g + 1)}
            if g:
                left = m_left[:, :, lanes].reshape(512, C)
                res = dot(m_right[:, :, : g * C].reshape(512, g * C), left, TN)
                blocks.update({(gj, g): res[gj * C : (gj + 1) * C] for gj in range(g)})
            for (gj, gi), block in blocks.items():
                jr, (ra, rb) = rows_of(gj)[0], rows_of(gi)
                for jh in range(2):
                    for jq in range(2):
                        at = jh * 64 + jq * 32
                        pack(block[at : at + 32], ra, rb, (jr >> 2) * 8 + jh * 4 + (jr & 1) * 2 + jq)
        for o in far_first(range(1, ND)):
            give_back(0, ret, me ^ o)
        ret[me] = back[me]

    def combine_incoming(recv, ret):
        def label(g):
            return b0 ^ (g % 2), y0 ^ (g // 2)

        def column(g, x, core):
            b, y = label(g)
            return x * 8 + (b ^ x) * 4 + y * 2 + core

        for g in range(GROUPS):
            wait_for(recv, MEMBERS - (g == 0), recv_sems.at[1, g])
            for x in range(2):
                for core in range(2):
                    for p in range(4):
                        assemble(recv, 2 * p, 2 * p + 1, column(g, x, core), g * 4 + x * 2 + core,
                                 slice(p * C, (p + 1) * C))
            right = m_right[g * 4 : (g + 1) * 4].reshape(C, 512)
            res = dot(right, m_left[: (g + 1) * 4].reshape((g + 1) * C, 512), NT)
            blocks = {(g, gi): res[:, gi * C : (gi + 1) * C] for gi in range(g + 1)}
            if g:
                left = m_left[g * 4 : (g + 1) * 4].reshape(C, 512)
                res = dot(m_right[: g * 4].reshape(g * C, 512), left, NT)
                blocks.update({(gj, g): res[gj * C : (gj + 1) * C] for gj in range(g)})
            sends = []
            for (gj, gi), block in blocks.items():
                b, y = label(gi)
                for x in range(2):
                    for core in range(2):
                        at = (x * 2 + core) * 32
                        pack(block[at : at + 32], b * 2 + y, 4 + (b ^ 1) * 2 + y, column(gj, x, core))
                for xr in range(2):
                    tr = (r >> 2) ^ xr
                    tr = tr * 4 + (tr ^ b) * 2 + y
                    for k in range(4):
                        o = (k // 2) * 8 + (k // 2 ^ gj % 2) * 4 + (gj // 2) * 2 + k % 2
                        sends.append((hops(o & 6) + k // 2, tr * NC + (q ^ o)))
            for _, peer in sorted(sends, key=lambda e: -e[0]):
                @pl.when(peer != me)
                def _(peer=peer):
                    give_back(1, ret, peer)
        ret[slot(1, me)] = back[me]

    def receive(l, ret):
        wait_for(ret, ND - 1, ret_sems.at[l])
        for t in range(8):
            stage[t * 256 : (t + 1) * 256, :] = ret[t * 16 : (t + 1) * 16].astype(F32).reshape(256, C)

    def normed_out(l, s):
        return norm_rows(stage[pl.ds(s, C, stride=16), :], cols[l, 1, 0], cols[l, 1, 1])

    turn_norm(0, 0)
    loads[0].wait()
    turn_weights(0)
    loads[1].wait()
    for t in range(8):
        first(t)
    project(0, 0)
    pl.semaphore_wait(barrier, MEMBERS - 1 + GROUPS - 1)
    for g in range(1, GROUPS):
        pl.semaphore_signal(in_sems.at[g], inc=1, device_id=place(me ^ group_bits(g)), device_id_type=MESH)
    send_groups(0, (0,), recv0)
    project(0, 1)
    pl.semaphore_wait(in_sems.at[1], 1)
    send_groups(0, (1,), recv0)
    project(0, 2)
    project(0, 3)
    pl.semaphore_wait(in_sems.at[2], 1)
    pl.semaphore_wait(in_sems.at[3], 1)
    send_groups(0, (2, 3), recv0)
    loads[2].wait()
    for l, i in ((0, 1), (1, 0), (1, 1)):
        turn_norm(l, i)
    for l in range(2):
        w_out_t[l] = w_out[l].T
    w_gate_t[...] = w_in[0, :, 4 * C :].T
    for t in range(CHUNKS):
        gate[t] = jax.nn.sigmoid(dot(w_gate_t[...], normed[:, t * C : (t + 1) * C], NN))
    turn_weights(1)
    combine_outgoing(recv0, ret0)
    wait_for(send, ND - 1, send_sems.at[0])
    receive(0, ret0)

    for s in range(CHUNKS):
        v = x[s] + gate[s] * dot(w_out_t[0], normed_out(0, s), NN)
        x[s] = v
        normed[:, s * C : (s + 1) * C] = norm_rows(v, cols[1, 0, 0], cols[1, 0, 1])
    project(1, 0)
    send_groups(1, (0,), recv1)
    for g in range(1, GROUPS):
        project(1, g)
    send_groups(1, (1, 2, 3), recv1)
    for s in range(CHUNKS):
        x_pos[s] = x[s].T
        gate[s] = jax.nn.sigmoid(dot(normed[:, s * C : (s + 1) * C], w_in[1, :, 4 * C :], TN))
    wait_for(back, ND - 1, back_sems.at[0])
    combine_incoming(recv1, ret1)
    wait_for(send, ND - 1, send_sems.at[1])
    receive(1, ret1)
    wait_for(back, ND - 1, back_sems.at[1])

    for s in range(CHUNKS):
        res = x_pos[s] + gate[s] * dot(normed_out(1, s), w_out[1], TN)
        for h in range(2):
            out[pl.ds(h * 16 + s, ROWS, stride=COLS), :] = res[h * ROWS : (h + 1) * ROWS]


def body(pair, token_mask, norm_gains, norm_biases, in_weights, out_weights):
    vmem = pl.BlockSpec(memory_space=pltpu.VMEM)
    hbm = pl.BlockSpec(memory_space=pltpu.HBM)
    res = pl.pallas_call(
        kernel,
        out_shape=jax.ShapeDtypeStruct((ROWS * COLS, C), F32),
        in_specs=[hbm] * 7,
        out_specs=vmem,
        scratch_shapes=[
            pltpu.VMEM((2048, C), F32),
            pltpu.SMEM((512,), jnp.int32),
            pltpu.VMEM((4, C), jnp.int32),
            pltpu.VMEM((4, C), F32),
            pltpu.VMEM((4, C), F32),
            pltpu.VMEM((2, C, 5 * C), BF16),
            pltpu.VMEM((2, C, C), BF16),
            pltpu.VMEM((CHUNKS, C, C), F32),
            pltpu.VMEM((CHUNKS, C, C), F32),
            pltpu.VMEM((C, 2048), BF16),
            pltpu.VMEM((CHUNKS, C, C), F32),
            pltpu.VMEM((2, GROUPS, C, C), BF16),
            pltpu.VMEM((C, C), BF16),
            pltpu.VMEM((2, C, C), BF16),
            pltpu.VMEM((8, 1, 256), F32),
            pltpu.VMEM((2, 2, 2, C, C), F32),
            pltpu.VMEM((ND, 32, C), BF16),
            pltpu.VMEM((ND, 32, C), BF16),
            pltpu.VMEM((ND, 32, C), BF16),
            pltpu.VMEM((ND, 16, C), BF16),
            pltpu.VMEM((ND, 16, C), BF16),
            pltpu.VMEM((ND, 16, C), BF16),
            pltpu.VMEM((2048, C), F32),
            pltpu.VMEM((NC, 32, 512), BF16),
            pltpu.VMEM((NC, 32, 512), BF16),
            pltpu.VMEM((2048, C), F32),
            pltpu.SemaphoreType.DMA((7,)),
            pltpu.SemaphoreType.REGULAR((GROUPS,)),
            pltpu.SemaphoreType.DMA((2,)),
            pltpu.SemaphoreType.DMA((2, GROUPS)),
            pltpu.SemaphoreType.DMA((2,)),
            pltpu.SemaphoreType.DMA((2,)),
        ],
        compiler_params=pltpu.CompilerParams(
            collective_id=0, has_side_effects=True, vmem_limit_bytes=48 << 20),
    )(
        pair.reshape(ROWS * COLS, C), token_mask, token_mask.reshape(4, C),
        norm_gains.reshape(4, C), norm_biases.reshape(4, C), in_weights, out_weights,
    )
    return res.reshape(ROWS, COLS, C)


def solution(mesh):
    placed = (P("row", "col", None), P(), P(), P(), P(), P())
    return jax.shard_map(
        body, mesh=mesh, in_specs=placed, out_specs=P("row", "col", None), check_vma=False
    )
```
